256 devices in a mesh: expert: 64 (over z, x_lo, y), dp: 4 (over x_hi, core).
Axes of the slice: x: 4 (x_hi: 2, x_lo: 2; x = x_hi * 2 + x_lo), y: 4, z: 8, core: 2. Of those that a mesh axis runs over, the one named last changes fastest.
Arguments:
- tokens: bfloat16 [32768, 2048], P(('expert', 'dp')), may hold values from -6 to 6
- cotangent: bfloat16 [32768, 2048], P(('expert', 'dp')), may hold values from -0.59765625 to 0.59765625
- routes: int32 [32768, 2], P(('expert', 'dp')), may hold values from 0 to 63, as said below
- combine: float32 [32768, 2], P(('expert', 'dp')), may hold values from 0.2 to 1
- counts: int32 [64], replicated, may hold values from 0 to 2999, as said below
- gate_weight: bfloat16 [64, 2048, 512], P('expert'), may hold values from -0.125 to 0.125
- up_weight: bfloat16 [64, 2048, 512], P('expert'), may hold values from -0.125 to 0.125
- down_weight: bfloat16 [64, 2048, 512], P('expert'), may hold values from -0.25 to 0.25
Outputs:
- mixed: bfloat16 [32768, 2048], P(('expert', 'dp'))
- input_grad: bfloat16 [32768, 2048], P(('expert', 'dp'))
- combine_grad: float32 [32768, 2], P(('expert', 'dp'))
- gate_grad: float32 [64, 2048, 512], P('expert', None, 'dp')
- up_grad: float32 [64, 2048, 512], P('expert', None, 'dp')
- down_grad: float32 [64, 2048, 512], P('expert', None, 'dp')
The draws below stay inside these ranges and needn't reach their ends.
Inputs may be any that keep to these rules, and one draw needn't show every extreme that they name: `counts`: the two largest entries are unique: no other expert has a count equal to either. `routes`: rows come in aligned blocks of 128, one block to a device. In a block the two experts of a row differ. One and the same expert other than the two with the largest counts is named exactly 4 + 4 // 2 times in every block; every other such expert at most 4 times. Each of the two with the largest counts is named at least 8 and at most 12 + 4 // 2 times in a block, and that most in some block.
All inputs are finite; a program needn't handle non-finite values.
Results may differ from the reference program's by a relative error of at most 0.0065.
Values may be sent and summed in bfloat16 or wider, within the bound.
No kernel may reach another device: no remote copies, remote signals or barrier semaphores. Data moves between devices by JAX's collectives and lax.ppermute only.
A program may use at most 128 MiB of HBM per device.

```python
import jax
import jax.numpy as jnp
from jax import lax

D = 2048
H = 512
TOK_DEV = 128
EXPERTS = 64
TOKENS = 32768
CAP = 4
HOT_CAP = 12
N_EXPERT = 64
N_DP = 4


def special_experts(key):
    shuffled = jax.random.permutation(jax.random.fold_in(key, 101), EXPERTS).astype(jnp.int32)
    return (shuffled[0], shuffled[1], shuffled[2])


def draw_counts(key, part):
    hottest, second, filled = special_experts(key)
    expert_ids = jnp.arange(EXPERTS, dtype=jnp.int32)
    drawn = jax.random.randint(jax.random.fold_in(key, 102), (EXPERTS,), 0, 1000, dtype=jnp.int32)
    hot_extra = jax.random.randint(jax.random.fold_in(key, 103), (2,), 0, 1000, dtype=jnp.int32)
    result = jnp.where(expert_ids == hottest, 2999, drawn)
    result = jnp.where(expert_ids == second, 1000 + hot_extra[1], result)
    result = jnp.where(expert_ids == filled, 0, result)
    return result.astype(jnp.int32)


def block_routes(block_key, hottest, second, filled, load_filled, load_hottest, load_second):
    expert_ids = jnp.arange(EXPERTS, dtype=jnp.int32)
    shuffled = jax.random.permutation(jax.random.fold_in(block_key, 1), EXPERTS).astype(jnp.int32)
    special = (shuffled == hottest) | (shuffled == second) | (shuffled == filled)
    ranking = jnp.where(special, EXPERTS + expert_ids, expert_ids)
    others = shuffled[jnp.argsort(ranking)]
    position = jnp.arange(2 * TOK_DEV, dtype=jnp.int32)
    leading_total = load_filled + load_hottest + load_second
    remainder = jnp.maximum(position - leading_total, 0) // CAP
    labels = others[jnp.minimum(remainder, EXPERTS - 4)]
    labels = jnp.where(position < leading_total, second, labels)
    labels = jnp.where(position < load_filled + load_hottest, hottest, labels)
    labels = jnp.where(position < load_filled, filled, labels)
    paired = jnp.stack([labels[:TOK_DEV], labels[TOK_DEV:]], axis=1)
    shuffle = jax.random.permutation(jax.random.fold_in(block_key, 2), TOK_DEV)
    paired = paired[shuffle]
    flipped = jax.random.randint(jax.random.fold_in(block_key, 3), (TOK_DEV, 1), 0, 2, dtype=jnp.int32)
    return jnp.where(flipped == 1, paired[:, ::-1], paired).astype(jnp.int32)


def draw_routes(key, part):
    hottest, second, filled = special_experts(key)
    blocks = TOKENS // TOK_DEV
    excess = CAP // 2
    hot_peak = HOT_CAP + excess
    first_raw = jax.random.randint(jax.random.fold_in(key, 104), (blocks,), 2 * CAP, hot_peak + 1, dtype=jnp.int32)
    second_raw = jax.random.randint(jax.random.fold_in(key, 107), (blocks,), 2 * CAP, hot_peak + 1, dtype=jnp.int32)
    peak_first = jax.random.randint(jax.random.fold_in(key, 105), (), 0, blocks, dtype=jnp.int32)
    offset = jax.random.randint(jax.random.fold_in(key, 108), (), 0, blocks - 1, dtype=jnp.int32)
    peak_second = (peak_first + 1 + offset) % blocks
    block_index = jnp.arange(blocks, dtype=jnp.int32)
    load_first = jnp.where(block_index == peak_first, hot_peak, jnp.where(block_index == peak_second, 2 * CAP, first_raw)).astype(jnp.int32)
    load_next = jnp.where(block_index == peak_second, hot_peak, jnp.minimum(second_raw, 6 * CAP - load_first)).astype(jnp.int32)
    load_filled = jnp.full((blocks,), CAP + excess, dtype=jnp.int32)
    block_keys = jax.random.split(jax.random.fold_in(key, 106), blocks)
    result = jax.vmap(lambda block_key, load_zero, load_one, load_two: block_routes(block_key, hottest, second, filled, load_zero, load_one, load_two))(block_keys, load_filled, load_first, load_next)
    return result.reshape(TOKENS, 2)


def block_levels(stream_key, extent, cuts, low, high):
    level = 1.0
    for dim, parts in cuts:
        heights = jax.random.uniform(jax.random.fold_in(jax.random.fold_in(stream_key, 6), dim), (parts,), jnp.float32, low / len(cuts), high / len(cuts))
        level = level * jnp.repeat(jnp.exp(heights), extent[dim] // parts).reshape((-1,) + (1,) * (len(extent) - 1 - dim))
    return level


def scatter_about(own_key, dims, scale, reach, cuts=(), held_as=jnp.bfloat16):
    gain = block_levels(own_key, dims, cuts, -0.22, 0.18) if cuts else 1.0
    values = jax.random.normal(own_key, dims, jnp.float32) * scale * gain
    return jnp.minimum(jnp.maximum(values, -reach), reach).astype(held_as)


def setup_inputs(seed: int = 0) -> dict:
    streams_of = jax.random.split(jax.random.key(seed), 9)
    return {
        "tokens": scatter_about(streams_of[0], (TOKENS, D), 1.0, 6.0, ((0, 256),)),
        "cotangent": scatter_about(streams_of[1], (TOKENS, D), 0.1, 0.59765625, ((0, 256),)),
        "routes": draw_routes(jax.random.fold_in(streams_of[8], 71), 0),
        "combine": jnp.clip(0.2 + 0.8 * jax.random.uniform(streams_of[3], (TOKENS, 2), jnp.float32) ** block_levels(streams_of[3], (TOKENS, 2), ((0, 256),), -0.2, 0.2), 0.2, 1.0),
        "counts": draw_counts(jax.random.fold_in(streams_of[8], 71), 0),
        "gate_weight": scatter_about(streams_of[5], (EXPERTS, D, H), D ** -0.5, 0.125, ((0, 64),)),
        "up_weight": scatter_about(streams_of[6], (EXPERTS, D, H), D ** -0.5, 0.125, ((0, 64),)),
        "down_weight": scatter_about(streams_of[7], (EXPERTS, D, H), H ** -0.5, 0.25, ((0, 64),)),
    }


def slot_owners(slot_index, slot_total, positions):
    matches = slot_index[None, :] == jnp.arange(slot_total, dtype=jnp.int32)[:, None]
    occupied = jnp.any(matches, axis=1)
    filler = jnp.sum(jnp.where(matches, positions[None, :], 0), axis=1).astype(jnp.int32)
    return filler, occupied


def route_plan(routes, hot_ids, experts, capacity, hot_cap):
    flat_routes = routes.reshape(-1).astype(jnp.int32)
    pair_count = flat_routes.shape[0]
    expert_ids = jnp.arange(experts, dtype=jnp.int32)
    onehot = (flat_routes[:, None] == expert_ids[None, :]).astype(jnp.int32)
    running = jnp.cumsum(onehot, axis=0).astype(jnp.int32)
    slot_rank = jnp.sum((running - onehot) * onehot, axis=1).astype(jnp.int32)
    leading = flat_routes == hot_ids[0]
    trailing = flat_routes == hot_ids[1]
    is_hot = leading | trailing
    keep_mask = slot_rank < jnp.where(is_hot, hot_cap, capacity)
    main_total = experts * capacity
    hot_total = 2 * hot_cap
    main_index = jnp.where(keep_mask & ~is_hot, flat_routes * capacity + slot_rank, main_total).astype(jnp.int32)
    hot_index = jnp.where(keep_mask & is_hot, jnp.where(leading, 0, hot_cap) + slot_rank, hot_total).astype(jnp.int32)
    assign = jnp.where(keep_mask, jnp.where(is_hot, main_total + hot_index, main_index), main_total + hot_total).astype(jnp.int32)
    positions = jnp.arange(pair_count, dtype=jnp.int32)
    main_fill, main_used = slot_owners(main_index, main_total, positions)
    hot_fill, hot_used = slot_owners(hot_index, hot_total, positions)
    return main_fill, main_used, hot_fill, hot_used, assign


def expert_forward(row_data, gate_weight, up_weight, down_weight):
    gate_value = jnp.dot(row_data, gate_weight, preferred_element_type=jnp.float32)
    up_value = jnp.dot(row_data, up_weight, preferred_element_type=jnp.float32)
    sigmoid_gate = jax.nn.sigmoid(gate_value)
    activation = (gate_value * sigmoid_gate * up_value).astype(jnp.bfloat16)
    output = lax.dot_general(activation, down_weight, (((1,), (1,)), ((), ())), preferred_element_type=jnp.float32)
    return (gate_value, up_value, sigmoid_gate, activation), output


def expert_backward(cot_rows, stored, gate_weight, up_weight, down_weight):
    gate_value, up_value, sigmoid_gate, activation = stored
    back_hidden = jnp.dot(cot_rows, down_weight, preferred_element_type=jnp.float32)
    gate_part = (back_hidden * up_value * sigmoid_gate * (1.0 + gate_value * (1.0 - sigmoid_gate))).astype(jnp.bfloat16)
    up_part = (back_hidden * gate_value * sigmoid_gate).astype(jnp.bfloat16)
    contract_last = (((1,), (1,)), ((), ()))
    input_part = lax.dot_general(gate_part, gate_weight, contract_last, preferred_element_type=jnp.float32) + lax.dot_general(up_part, up_weight, contract_last, preferred_element_type=jnp.float32)
    return gate_part, up_part, input_part


def weight_grads(row_data, cot_rows, activation, gate_part, up_part):
    contract_rows = (((0,), (0,)), ((), ()))
    return jnp.stack([
        lax.dot_general(row_data, gate_part, contract_rows, preferred_element_type=jnp.float32),
        lax.dot_general(row_data, up_part, contract_rows, preferred_element_type=jnp.float32),
        lax.dot_general(cot_rows, activation, contract_rows, preferred_element_type=jnp.float32)])


def run_expert(row_data, cot_rows, gate_weight, up_weight, down_weight):
    stored, output = expert_forward(row_data, gate_weight, up_weight, down_weight)
    gate_part, up_part, input_part = expert_backward(cot_rows, stored, gate_weight, up_weight, down_weight)
    grads = weight_grads(row_data, cot_rows, stored[3], gate_part, up_part)
    return output.astype(jnp.bfloat16), input_part.astype(jnp.bfloat16), grads


def reference(tokens, cotangent, routes, combine, counts, gate_weight, up_weight, down_weight):
    devices = N_EXPERT * N_DP
    model_width = tokens.shape[1]
    hot_ids = lax.top_k(counts, 2)[1].astype(jnp.int32)
    main_fill, main_used, hot_fill, hot_used, assign = jax.vmap(
        lambda block: route_plan(block, hot_ids, EXPERTS, CAP, HOT_CAP))(routes.reshape(devices, TOK_DEV, 2))
    flat_combine = combine.reshape(devices, 2 * TOK_DEV)
    block_start = (jnp.arange(devices, dtype=jnp.int32) * TOK_DEV)[:, None]
    zero_value = jnp.zeros((), jnp.bfloat16)

    def gather_rows(filler, occupied):
        token_index = (block_start + filler // 2).reshape(-1).astype(jnp.int32)
        picked = jnp.take_along_axis(flat_combine, filler, axis=1).reshape(-1)
        row_mask = occupied.reshape(-1)[:, None]
        row_data = jnp.where(row_mask, tokens[token_index], zero_value)
        scaled = (picked[:, None] * cotangent[token_index].astype(jnp.float32)).astype(jnp.bfloat16)
        return row_data, jnp.where(row_mask, scaled, zero_value)

    def one_expert(expert):
        start = (expert * CAP).astype(jnp.int32)
        filler = lax.dynamic_slice_in_dim(main_fill, start, CAP, 1)
        occupied = lax.dynamic_slice_in_dim(main_used, start, CAP, 1)
        row_data, cot_rows = gather_rows(filler, occupied)
        return run_expert(row_data, cot_rows, gate_weight[expert], up_weight[expert], down_weight[expert])

    main_out, main_input, grads = lax.map(one_expert, jnp.arange(EXPERTS, dtype=jnp.int32))
    hot_out = []
    hot_input = []
    for member in range(2):
        row_data, cot_rows = gather_rows(hot_fill[:, member * HOT_CAP:(member + 1) * HOT_CAP],
                                         hot_used[:, member * HOT_CAP:(member + 1) * HOT_CAP])
        chosen = hot_ids[member]
        output, input_part, hot_grads = run_expert(row_data, cot_rows, gate_weight[chosen], up_weight[chosen], down_weight[chosen])
        hot_out.append(output)
        hot_input.append(input_part)
        grads = grads.at[chosen].add(hot_grads)

    device_ids = jnp.arange(devices, dtype=jnp.int32)[:, None]
    main_total = EXPERTS * CAP
    main_pos = (assign // CAP) * (devices * CAP) + device_ids * CAP + assign % CAP
    hot_local = assign - main_total
    hot_pos = EXPERTS * devices * CAP + (hot_local // HOT_CAP) * (devices * HOT_CAP) + device_ids * HOT_CAP + hot_local % HOT_CAP
    row_total = EXPERTS * devices * CAP + 2 * devices * HOT_CAP
    row_index = jnp.where(assign < main_total, main_pos,
                          jnp.where(assign == main_total + 2 * HOT_CAP, row_total, hot_pos)).reshape(-1).astype(jnp.int32)
    zero_row = jnp.zeros((1, model_width), jnp.bfloat16)
    out_table = jnp.concatenate([main_out.reshape(-1, model_width), hot_out[0], hot_out[1], zero_row], axis=0)
    input_table = jnp.concatenate([main_input.reshape(-1, model_width), hot_input[0], hot_input[1], zero_row], axis=0)
    out_each = out_table[row_index].reshape(TOKENS, 2, model_width).astype(jnp.float32)
    mixed = jnp.sum(combine[:, :, None] * out_each, axis=1).astype(jnp.bfloat16)
    combine_grad = jnp.sum(out_each * cotangent.astype(jnp.float32)[:, None, :], axis=2)
    input_each = input_table[row_index].reshape(TOKENS, 2, model_width).astype(jnp.float32)
    input_grad = jnp.sum(input_each, axis=1).astype(jnp.bfloat16)
    return mixed, input_grad, combine_grad, grads[:, 0], grads[:, 1], grads[:, 2]
```

```python
import functools

import jax
import jax.numpy as jnp
from jax import lax
from jax.experimental import pallas as pl
from jax.experimental.pallas import tpu as pltpu
from jax.sharding import Mesh
from jax.sharding import PartitionSpec as P

D = 2048
H = 512
TOK = 128
EXPERTS = 64
CAP = 4
HOT_CAP = 12
SLOT = 2 * CAP
SENT = EXPERTS * SLOT
PAIR = 2 * HOT_CAP
SHARE = 128
WROWS = 3 * D
NZ, NXL, NY, NXH, NC = 8, 2, 4, 2, 2
ALL = ("z", "xl", "y", "xh", "c")
E = ("z", "xl", "y")
X = ("xh", "xl")
BF = jnp.bfloat16
F32 = jnp.float32
MIB = 1024 * 1024


def contract(a, b, da, db):
    return lax.dot_general(a, b, (((da,), (db,)), ((), ())), preferred_element_type=F32)


def iota(shape, dim):
    return lax.broadcasted_iota(jnp.int32, shape, dim)


def cost(flops, nbytes):
    return pl.CostEstimate(flops=int(flops), bytes_accessed=int(nbytes), transcendentals=0)


def whole(space=pltpu.VMEM):
    return pl.BlockSpec(memory_space=space)


def pack_kernel(core_ref, counts_ref, routes_ref, combine_ref, tokens_ref, cot_ref,
                send_ref, mine_ref, theirs_ref, slots_ref):
    core = core_ref[0]
    counts = counts_ref[...].astype(F32)
    ids = iota((1, EXPERTS), 1).astype(F32)
    low = jnp.float32(-3.0e38)

    def largest(values):
        top = jnp.max(values, axis=1, keepdims=True)
        return jnp.min(jnp.where(values == top, ids, float(EXPERTS)), axis=1, keepdims=True)

    hot0 = largest(counts)
    hot1 = largest(jnp.where(ids == hot0, low, counts))
    eid = iota((EXPERTS, TOK), 0)
    routes = [routes_ref[k:k + 1, :] for k in range(2)]
    weight = [combine_ref[k:k + 1, :] for k in range(2)]
    oh = [(eid == r).astype(F32) for r in routes]
    earlier = (iota((TOK, TOK), 0) < iota((TOK, TOK), 1)).astype(F32).astype(BF)
    cum = jnp.dot((oh[0] + oh[1]).astype(BF), earlier, preferred_element_type=F32)
    rank = [jnp.sum(cum * oh[0], axis=0, keepdims=True),
            jnp.sum((cum + oh[0]) * oh[1], axis=0, keepdims=True)]
    main, mine, theirs = [], [], []
    for k in range(2):
        rf = routes[k].astype(F32)
        lead = rf == hot0
        hot = lead | (rf == hot1)
        member = jnp.where(lead, 0, 1)
        r = rank[k].astype(jnp.int32)
        keep = r < jnp.where(hot, HOT_CAP, CAP)
        main.append(jnp.where(keep & jnp.logical_not(hot), routes[k] * SLOT + r, -1))
        mine.append(jnp.where(keep & hot & (member == core), r, -1))
        theirs.append(jnp.where(keep & hot & (member != core), r, -1))
        slots_ref[k:k + 1, :] = jnp.where(
            main[k] >= 0, main[k],
            jnp.where(mine[k] >= 0, SENT + mine[k], jnp.where(theirs[k] >= 0, SENT + PAIR + theirs[k], -1)))

    def rows(slot, shift, base, count):
        sid = iota((count, TOK), 0) + base
        at = [jnp.where(s >= 0, s + shift, -1) for s in slot]
        hit = [sid == s for s in slot]
        hit_c = [sid == a for a in at]
        pick = (hit[0] | hit[1]).astype(F32).astype(BF)
        pick_c = (hit_c[0] | hit_c[1]).astype(F32).astype(BF)
        w = jnp.sum(jnp.where(hit_c[0], weight[0], 0.0) + jnp.where(hit_c[1], weight[1], 0.0),
                    axis=1, keepdims=True)
        data = jnp.dot(pick, tokens_ref[...], preferred_element_type=F32)
        cot = jnp.dot(pick_c, cot_ref[...], preferred_element_type=F32)
        return (data + w * cot).astype(BF)

    mine_ref[...] = rows(mine, HOT_CAP, 0, PAIR)
    theirs_ref[...] = rows(theirs, HOT_CAP, 0, PAIR)
    step = 128

    def body(i, carry):
        base = pl.multiple_of(i * step, step)
        send_ref[pl.ds(base, step), :] = rows(main, CAP, base, step)
        return carry

    lax.fori_loop(0, SENT // step, body, 0)


def pack(core, counts, routes_t, combine_t, tokens, cotangent):
    return pl.pallas_call(
        pack_kernel,
        out_shape=(jax.ShapeDtypeStruct((SENT, D), BF), jax.ShapeDtypeStruct((PAIR, D), BF),
                   jax.ShapeDtypeStruct((PAIR, D), BF), jax.ShapeDtypeStruct((2, TOK), jnp.int32)),
        in_specs=[whole(pltpu.SMEM)] + [whole()] * 5,
        out_specs=(whole(),) * 4,
        compiler_params=pltpu.CompilerParams(vmem_limit_bytes=32 * MIB),
        cost_estimate=cost(4 * SENT * TOK * D, 4 * SENT * D),
        name="pack",
    )(core, counts, routes_t, combine_t, tokens, cotangent)


def backward_parts(gate, up, back):
    s = jax.nn.sigmoid(gate)
    act = (gate * s * up).astype(BF)
    gate_part = (back * up * s * (1.0 + gate * (1.0 - s))).astype(BF)
    up_part = (back * gate * s).astype(BF)
    return gate_part, up_part, act


def expert_kernel(got_ref, gate_ref, up_ref, down_ref, back_ref, data_ref, cot_ref, parts_ref):
    count = EXPERTS * CAP
    i, j = iota((count, SENT), 0), iota((count, SENT), 1)
    at = (i >> 2) * SLOT + (i & 3)
    data_ref[...] = jnp.dot((j == at).astype(F32).astype(BF), got_ref[...], preferred_element_type=F32).astype(BF)
    cot_ref[...] = jnp.dot((j == at + CAP).astype(F32).astype(BF), got_ref[...], preferred_element_type=F32).astype(BF)
    data, cot = data_ref[...], cot_ref[...]
    gate = jnp.dot(data, gate_ref[0], preferred_element_type=F32)
    up = jnp.dot(data, up_ref[0], preferred_element_type=F32)
    back = jnp.dot(cot, down_ref[0], preferred_element_type=F32)
    gate_part, up_part, act = backward_parts(gate, up, back)
    for m, part in enumerate((gate_part, up_part, act)):
        for q in range(H // SHARE):
            parts_ref[m, q] = part[:, q * SHARE:(q + 1) * SHARE]
    out = contract(act, down_ref[0], 1, 1).astype(BF)
    inp = (contract(gate_part, gate_ref[0], 1, 1) + contract(up_part, up_ref[0], 1, 1)).astype(BF)
    i, j = iota((SENT, count), 1), iota((SENT, count), 0)
    at = (i >> 2) * SLOT + (i & 3)
    back_ref[...] = (jnp.dot((j == at).astype(F32).astype(BF), out, preferred_element_type=F32)
                     + jnp.dot((j == at + CAP).astype(F32).astype(BF), inp, preferred_element_type=F32)).astype(BF)


def run_expert(got, gate_weight, up_weight, down_weight):
    count = EXPERTS * CAP
    return pl.pallas_call(
        expert_kernel,
        out_shape=(jax.ShapeDtypeStruct((SENT, D), BF), jax.ShapeDtypeStruct((count, D), BF),
                   jax.ShapeDtypeStruct((count, D), BF),
                   jax.ShapeDtypeStruct((3, H // SHARE, count, SHARE), BF)),
        in_specs=[whole()] * 4,
        out_specs=(whole(),) * 4,
        compiler_params=pltpu.CompilerParams(vmem_limit_bytes=48 * MIB),
        cost_estimate=cost(12 * count * D * H + 8 * SENT * count * D, 12 * MIB),
        name="expert",
    )(got, gate_weight, up_weight, down_weight)


def grads_kernel(core_ref, data_ref, cot_ref, parts_ref, keep_ref, send_ref):
    core = core_ref[0]
    order = (core, 2 + core, 1 - core, 3 - core)
    pick = [[parts_ref[m, q] for q in order] for m in range(3)]
    first = contract(data_ref[...], jnp.concatenate(pick[0] + pick[1], axis=1), 0, 0)
    second = contract(cot_ref[...], jnp.concatenate(pick[2], axis=1), 0, 0)
    for m in range(3):
        for n in range(4):
            at = ((m * 4 + n) if m < 2 else n) * SHARE
            value = (first if m < 2 else second)[:, at:at + SHARE]
            if n < 2:
                keep_ref[n, m] = value
            else:
                send_ref[n - 2, m] = value.astype(BF)


def main_grads(core, data, cot, parts):
    count = EXPERTS * CAP
    block = 512
    return pl.pallas_call(
        grads_kernel,
        grid=(D // block,),
        out_shape=(jax.ShapeDtypeStruct((2, 3, D, SHARE), F32), jax.ShapeDtypeStruct((2, 3, D, SHARE), BF)),
        in_specs=[whole(pltpu.SMEM),
                  pl.BlockSpec((count, block), lambda i: (0, i)),
                  pl.BlockSpec((count, block), lambda i: (0, i)),
                  pl.BlockSpec((3, H // SHARE, count, SHARE), lambda i: (0, 0, 0, 0))],
        out_specs=(pl.BlockSpec((2, 3, block, SHARE), lambda i: (0, 0, i, 0)),
                   pl.BlockSpec((2, 3, block, SHARE), lambda i: (0, 0, i, 0))),
        compiler_params=pltpu.CompilerParams(vmem_limit_bytes=40 * MIB),
        cost_estimate=cost(6 * count * D * H, 12 * MIB),
        name="main_grads",
    )(core, data, cot, parts)


def hot_kernel(rows_ref, weights_ref, ret_ref, grads_ref):
    total = NXH * NXL * 2 * PAIR
    count = total // 2

    def place(i):
        group = jnp.floor((i.astype(F32) + 0.5) * (1.0 / HOT_CAP)).astype(jnp.int32)
        return group * HOT_CAP + i

    i, j = iota((count, total), 0), iota((count, total), 1)
    at = place(i)
    data = jnp.dot((j == at).astype(F32).astype(BF), rows_ref[...], preferred_element_type=F32).astype(BF)
    cot = jnp.dot((j == at + HOT_CAP).astype(F32).astype(BF), rows_ref[...], preferred_element_type=F32).astype(BF)
    gate_w, up_w, down_w = (weights_ref[m * D:(m + 1) * D, :] for m in range(3))
    gate = jnp.dot(data, gate_w, preferred_element_type=F32)
    up = jnp.dot(data, up_w, preferred_element_type=F32)
    back = jnp.dot(cot, down_w, preferred_element_type=F32)
    gate_part, up_part, act = backward_parts(gate, up, back)
    out = contract(act, down_w, 1, 1).astype(BF)
    inp = (contract(gate_part, gate_w, 1, 1) + contract(up_part, up_w, 1, 1)).astype(BF)
    i, j = iota((total, count), 1), iota((total, count), 0)
    at = place(i)
    ret_ref[...] = (jnp.dot((j == at).astype(F32).astype(BF), out, preferred_element_type=F32)
                    + jnp.dot((j == at + HOT_CAP).astype(F32).astype(BF), inp, preferred_element_type=F32)).astype(BF)
    grads_ref[0:D, :] = contract(data, gate_part, 0, 0).astype(BF)
    grads_ref[D:2 * D, :] = contract(data, up_part, 0, 0).astype(BF)
    grads_ref[2 * D:3 * D, :] = contract(cot, act, 0, 0).astype(BF)


def run_hot(rows, weights):
    return pl.pallas_call(
        hot_kernel,
        out_shape=(jax.ShapeDtypeStruct(rows.shape, BF), jax.ShapeDtypeStruct((WROWS, SHARE), BF)),
        in_specs=[whole()] * 2,
        out_specs=(whole(),) * 2,
        compiler_params=pltpu.CompilerParams(vmem_limit_bytes=40 * MIB),
        cost_estimate=cost(18 * 96 * D * SHARE, 5 * MIB),
        name="hot",
    )(rows, weights)


def combine_kernel(back_ref, mine_ref, theirs_ref, slots_ref, combine_ref, cot_ref,
                   mixed_ref, input_ref, cgrad_ref):
    slot = [slots_ref[:, k:k + 1] for k in range(2)]

    def pick(base, count, shift):
        lane = iota((TOK, count), 1) + (base - shift)
        inside = iota((TOK, count), 1) >= shift
        return [jnp.where((lane == s) & (s >= base) & inside, 1.0, 0.0) for s in slot]

    tables = ((back_ref, 0, SENT, CAP), (mine_ref, SENT, PAIR, HOT_CAP), (theirs_ref, SENT + PAIR, PAIR, HOT_CAP))
    outs = []
    for k in range(2):
        total = None
        for ref, base, count, shift in tables:
            term = jnp.dot(pick(base, count, 0)[k].astype(BF), ref[...], preferred_element_type=F32)
            total = term if total is None else total + term
        outs.append(total)
    total = None
    for ref, base, count, shift in tables:
        both = pick(base, count, shift)
        term = jnp.dot((both[0] + both[1]).astype(BF), ref[...], preferred_element_type=F32)
        total = term if total is None else total + term
    input_ref[...] = total.astype(BF)
    mixed_ref[...] = (combine_ref[:, 0:1] * outs[0] + combine_ref[:, 1:2] * outs[1]).astype(BF)
    cot = cot_ref[...].astype(F32)
    for k in range(2):
        cgrad_ref[:, k:k + 1] = jnp.sum(outs[k] * cot, axis=1, keepdims=True)


def combine_rows(back, mine, theirs, slots, combine, cotangent):
    return pl.pallas_call(
        combine_kernel,
        out_shape=(jax.ShapeDtypeStruct((TOK, D), BF), jax.ShapeDtypeStruct((TOK, D), BF),
                   jax.ShapeDtypeStruct((TOK, 2), F32)),
        in_specs=[whole()] * 6,
        out_specs=(whole(),) * 3,
        compiler_params=pltpu.CompilerParams(vmem_limit_bytes=32 * MIB),
        cost_estimate=cost(6 * TOK * SENT * D, 4 * MIB),
        name="combine",
    )(back, mine, theirs, slots, combine, cotangent)


def exchange(x, axes):
    return lax.all_to_all(x, axes, split_axis=0, concat_axis=0, tiled=True)


def swap(x, axis):
    return lax.ppermute(x, axis, [(0, 1), (1, 0)])


def in_core_order(own, other, core):
    first = core == 0
    return jnp.where(first, own, other), jnp.where(first, other, own)


def hot_weights(gate_weight, up_weight, down_weight, roots, core, xh):
    stacked = [
        jnp.concatenate([lax.dynamic_slice_in_dim(w[0], (2 * xh + xl) * SHARE, SHARE, 1)
                         for w in (gate_weight, up_weight, down_weight)], axis=0)
        .reshape(NZ, NY, 2, WROWS // 64, SHARE)
        for xl in range(NXL)
    ]
    halves = [lax.dynamic_index_in_dim(s, core, 2, keepdims=False) for s in stacked]
    sent = jnp.stack(halves, axis=1).reshape(WROWS, SHARE)
    got = exchange(sent, E).reshape(EXPERTS, WROWS // 64, SHARE)
    own = lax.dynamic_index_in_dim(got, jnp.where(core == 0, roots[0], roots[1]), 0, keepdims=False)
    other = lax.dynamic_index_in_dim(got, jnp.where(core == 0, roots[1], roots[0]), 0, keepdims=False)
    first, second = in_core_order(own, swap(other, "c"), core)
    piece = jnp.concatenate([first, second], axis=0)
    piece = lax.all_gather(piece, "y", axis=0, tiled=True)
    return lax.all_gather(piece, "z", axis=0, tiled=True)


def reduce_over(x, axis, size):
    parts = exchange(x, axis).reshape(size, -1, SHARE)
    return jnp.sum(parts.astype(F32), axis=0)


def hot_grads_home(grads, roots, core):
    part = reduce_over(grads, "y", NY).astype(BF)
    part = reduce_over(part, "z", NZ).astype(BF).reshape(2, WROWS // 64, SHARE)
    own = lax.dynamic_index_in_dim(part, core, 0, keepdims=False)
    other = swap(lax.dynamic_index_in_dim(part, 1 - core, 0, keepdims=False), "c")
    dest = iota((EXPERTS, 1, 1), 0)
    mine = jnp.where(core == 0, roots[0], roots[1])
    theirs = jnp.where(core == 0, roots[1], roots[0])
    zero = jnp.zeros((), BF)
    sent = jnp.where(dest == mine, own[None], jnp.where(dest == theirs, other[None], zero))
    got = exchange(sent.reshape(WROWS, SHARE), E).reshape(NZ, NXL, NY, WROWS // 64, SHARE)
    keep = lax.dynamic_index_in_dim(got, core, 1, keepdims=False)
    give = swap(lax.dynamic_index_in_dim(got, 1 - core, 1, keepdims=False), "c")
    first, second = in_core_order(keep, give, core)
    both = jnp.stack([first, second], axis=2)
    return jnp.transpose(both, (1, 0, 2, 3, 4)).reshape(3, D, SHARE).astype(F32)


def per_device(tokens, cotangent, routes, combine, counts, gate_weight, up_weight, down_weight):
    core = lax.axis_index("c")
    xh = lax.axis_index("xh")
    core_arg = core.astype(jnp.int32).reshape(1)
    ids = jnp.arange(EXPERTS, dtype=jnp.int32)
    root0 = jnp.argmax(counts).astype(jnp.int32)
    root1 = jnp.argmax(jnp.where(ids == root0, jnp.iinfo(jnp.int32).min, counts)).astype(jnp.int32)
    roots = (root0, root1)

    weights = hot_weights(gate_weight, up_weight, down_weight, roots, core, xh)
    send, mine, theirs, slots = pack(core_arg, counts.reshape(1, EXPERTS), routes.T, combine.T, tokens, cotangent)
    got = exchange(send, E)
    hot_rows = jnp.concatenate([mine, swap(theirs, "c")], axis=0)
    hot_rows = lax.all_gather(hot_rows, X, axis=0, tiled=True)

    back, data, cot, parts = run_expert(got, gate_weight, up_weight, down_weight)
    back = exchange(back, E)

    ret, shadow = run_hot(hot_rows, weights)
    ret = exchange(ret, X).reshape(NXH * NXL, 2, PAIR, D)
    ret = jnp.sum(ret.astype(F32), axis=0).astype(BF)
    hot_mine = ret[0]
    hot_theirs = swap(ret[1], "c")

    keep, give = main_grads(core_arg, data, cot, parts)
    half = keep + swap(give, "c").astype(F32)
    part = lax.dynamic_index_in_dim(half, xh, 0, keepdims=False)
    other = swap(lax.dynamic_index_in_dim(half, 1 - xh, 0, keepdims=False).astype(BF), "xh")

    shadow = hot_grads_home(shadow, roots, core)
    grads = part + other.astype(F32) + shadow

    mixed, input_grad, combine_grad = combine_rows(back, hot_mine, hot_theirs, slots.T, combine, cotangent)
    return mixed, input_grad, combine_grad, grads[0][None], grads[1][None], grads[2][None]


def solution(mesh):
    split = Mesh(mesh.devices.reshape(NZ, NXL, NY, NXH, NC), ALL)
    rows = P(ALL, None)
    owned = P(E, None, None)
    grads = P(E, None, ("xh", "c"))
    return jax.shard_map(
        per_device,
        mesh=split,
        in_specs=(rows, rows, rows, rows, P(), owned, owned, owned),
        out_specs=(rows, rows, rows, grads, grads, grads),
        check_vma=False,
    )
```

```python
import functools

import jax
import jax.numpy as jnp
from jax import lax
from jax.experimental import pallas as pl
from jax.experimental.pallas import tpu as pltpu
from jax.sharding import Mesh
from jax.sharding import PartitionSpec as P

D = 2048
H = 512
TOK = 128
EXPERTS = 64
CAP = 4
HOT_CAP = 12
SLOT = 2 * CAP
SENT = EXPERTS * SLOT
PAIR = 2 * HOT_CAP
SHARE = 128
WROWS = 3 * D
NZ, NXL, NY, NXH, NC = 8, 2, 4, 2, 2
ALL = ("z", "xl", "y", "xh", "c")
E = ("z", "xl", "y")
X = ("xl", "xh")
S = ("xl", "y")
HALF = D // 2
PIECE = 32
BF = jnp.bfloat16
F32 = jnp.float32
MIB = 1024 * 1024


def contract(a, b, da, db):
    return lax.dot_general(a, b, (((da,), (db,)), ((), ())), preferred_element_type=F32)


def iota(shape, dim):
    return lax.broadcasted_iota(jnp.int32, shape, dim)


def cost(flops, nbytes):
    return pl.CostEstimate(flops=int(flops), bytes_accessed=int(nbytes), transcendentals=0)


def whole(space=pltpu.VMEM):
    return pl.BlockSpec(memory_space=space)


def scalars(*values):
    return jnp.stack([jnp.asarray(v, jnp.int32) for v in values])


def call(kernel, name, out, args, flops=0, moved=2 * MIB, vmem=24):
    return pl.pallas_call(
        kernel,
        out_shape=tuple(jax.ShapeDtypeStruct(shape, dtype) for shape, dtype in out),
        in_specs=[whole(pltpu.SMEM) if a.ndim == 1 else whole() for a in args],
        out_specs=(whole(),) * len(out),
        compiler_params=pltpu.CompilerParams(vmem_limit_bytes=vmem * MIB),
        cost_estimate=cost(flops, moved),
        name=name,
    )(*args)


def onehot(mask):
    return mask.astype(F32).astype(BF)


def pack_kernel(at_ref, counts_ref, routes_ref, combine_ref, tokens_ref, cot_ref,
                data_ref, scaled_ref, mine_ref, theirs_ref, slots_ref):
    core = at_ref[0]
    counts = counts_ref[...].astype(F32)
    ids = iota((1, EXPERTS), 1).astype(F32)
    low = jnp.float32(-3.0e38)

    def largest(values):
        top = jnp.max(values, axis=1, keepdims=True)
        return jnp.min(jnp.where(values == top, ids, float(EXPERTS)), axis=1, keepdims=True)

    hot0 = largest(counts)
    hot1 = largest(jnp.where(ids == hot0, low, counts))
    eid = iota((EXPERTS, TOK), 0)
    routes = [routes_ref[k:k + 1, :] for k in range(2)]
    weight = [combine_ref[k:k + 1, :] for k in range(2)]
    oh = [(eid == r).astype(F32) for r in routes]
    earlier = onehot(iota((TOK, TOK), 0) < iota((TOK, TOK), 1))
    cum = jnp.dot((oh[0] + oh[1]).astype(BF), earlier, preferred_element_type=F32)
    rank = [jnp.sum(cum * oh[0], axis=0, keepdims=True),
            jnp.sum((cum + oh[0]) * oh[1], axis=0, keepdims=True)]
    main, mine, theirs = [], [], []
    for k in range(2):
        rf = routes[k].astype(F32)
        lead = rf == hot0
        hot = lead | (rf == hot1)
        member = jnp.where(lead, 0, 1)
        r = rank[k].astype(jnp.int32)
        keep = r < jnp.where(hot, HOT_CAP, CAP)
        main.append(jnp.where(keep & jnp.logical_not(hot), routes[k] * SLOT + r, -1))
        mine.append(jnp.where(keep & hot & (member == core), r, -1))
        theirs.append(jnp.where(keep & hot & (member != core), r, -1))
        slots_ref[k:k + 1, :] = jnp.where(
            main[k] >= 0, main[k],
            jnp.where(mine[k] >= 0, SENT + mine[k], jnp.where(theirs[k] >= 0, SENT + PAIR + theirs[k], -1)))

    def hits(slot, shift, base, count):
        sid = iota((count, TOK), 0) + base
        hit = [sid == jnp.where(s >= 0, s + shift, -1) for s in slot]
        w = jnp.sum(jnp.where(hit[0], weight[0], 0.0) + jnp.where(hit[1], weight[1], 0.0), axis=1, keepdims=True)
        return onehot(hit[0] | hit[1]), w

    def hot_rows(slot):
        pick, _ = hits(slot, 0, 0, PAIR)
        pick_c, w = hits(slot, HOT_CAP, 0, PAIR)
        return (jnp.dot(pick, tokens_ref[...], preferred_element_type=F32)
                + w * jnp.dot(pick_c, cot_ref[...], preferred_element_type=F32)).astype(BF)

    mine_ref[...] = hot_rows(mine)
    theirs_ref[...] = hot_rows(theirs)
    step = 128

    def body(i, carry):
        base = pl.multiple_of(i * step, step)
        left, w_left = hits(main, 0, base, step)
        right, w_right = hits(main, CAP, base, step)
        data_ref[pl.ds(base, step), :] = (
            jnp.dot(left, tokens_ref[:, :HALF], preferred_element_type=F32)
            + jnp.dot(right, tokens_ref[:, HALF:], preferred_element_type=F32)).astype(BF)
        scaled_ref[pl.ds(base, step), :] = (
            w_left * jnp.dot(left, cot_ref[:, :HALF], preferred_element_type=F32)
            + w_right * jnp.dot(right, cot_ref[:, HALF:], preferred_element_type=F32)).astype(BF)
        return carry

    lax.fori_loop(0, SENT // step, body, 0)


def pack(at, counts, routes_t, combine_t, tokens, cotangent):
    out = [((SENT, HALF), BF), ((SENT, HALF), BF), ((PAIR, D), BF), ((PAIR, D), BF), ((2, TOK), jnp.int32)]
    return call(pack_kernel, "pack", out, (at, counts, routes_t, combine_t, tokens, cotangent),
                4 * SENT * TOK * D, 4 * SENT * D, 32)


def gather_halves(got_ref, rows_ref):
    count = EXPERTS * CAP
    i, j = iota((count, SENT), 0), iota((count, SENT), 1)
    at = (i >> 2) * SLOT + (i & 3)
    for h in range(2):
        rows_ref[:, h * HALF:(h + 1) * HALF] = jnp.dot(
            onehot(j == at + h * CAP), got_ref[...], preferred_element_type=F32).astype(BF)


def spread_halves(rows, out_ref):
    count = EXPERTS * CAP
    i, j = iota((SENT, count), 1), iota((SENT, count), 0)
    at = (i >> 2) * SLOT + (i & 3)
    out_ref[...] = (jnp.dot(onehot(j == at), rows[:, :HALF], preferred_element_type=F32)
                    + jnp.dot(onehot(j == at + CAP), rows[:, HALF:], preferred_element_type=F32)).astype(BF)


def forward_kernel(got_ref, gate_ref, up_ref, down_ref, out_ref, data_ref, gate_out, up_out, act_ref):
    gather_halves(got_ref, data_ref)
    data = data_ref[...]
    gate = jnp.dot(data, gate_ref[0], preferred_element_type=F32)
    up = jnp.dot(data, up_ref[0], preferred_element_type=F32)
    act = (gate * jax.nn.sigmoid(gate) * up).astype(BF)
    gate_out[...] = gate
    up_out[...] = up
    for q in range(H // SHARE):
        act_ref[q] = act[:, q * SHARE:(q + 1) * SHARE]
    spread_halves(contract(act, down_ref[0], 1, 1).astype(BF), out_ref)


def backward_parts(gate, up, back):
    s = jax.nn.sigmoid(gate)
    gate_part = (back * up * s * (1.0 + gate * (1.0 - s))).astype(BF)
    up_part = (back * gate * s).astype(BF)
    return gate_part, up_part


def backward_kernel(got_ref, gate_in, up_in, gate_ref, up_ref, down_ref, out_ref, cot_ref, parts_ref):
    gather_halves(got_ref, cot_ref)
    back = jnp.dot(cot_ref[...], down_ref[0], preferred_element_type=F32)
    gate_part, up_part = backward_parts(gate_in[...], up_in[...], back)
    for m, part in enumerate((gate_part, up_part)):
        for q in range(H // SHARE):
            parts_ref[m, q] = part[:, q * SHARE:(q + 1) * SHARE]
    spread_halves((contract(gate_part, gate_ref[0], 1, 1) + contract(up_part, up_ref[0], 1, 1)).astype(BF), out_ref)


def expert_forward(got, weights):
    count = EXPERTS * CAP
    out = [((SENT, HALF), BF), ((count, D), BF), ((count, H), F32), ((count, H), F32),
           ((H // SHARE, count, SHARE), BF)]
    return call(forward_kernel, "forward", out, (got,) + weights, 6 * count * D * H, 10 * MIB, 40)


def expert_backward(got, gate, up, weights):
    count = EXPERTS * CAP
    out = [((SENT, HALF), BF), ((count, D), BF), ((2, H // SHARE, count, SHARE), BF)]
    return call(backward_kernel, "backward", out, (got, gate, up) + weights, 6 * count * D * H, 10 * MIB, 40)


def grads_kernel(at_ref, data_ref, cot_ref, parts_ref, act_ref, keep_ref, send_ref):
    core = at_ref[0]
    order = (core, 2 + core, 1 - core, 3 - core)
    first = contract(data_ref[...], jnp.concatenate([parts_ref[m, q] for m in range(2) for q in order], axis=1), 0, 0)
    second = contract(cot_ref[...], jnp.concatenate([act_ref[q] for q in order], axis=1), 0, 0)
    for m in range(3):
        for n in range(4):
            at = ((m * 4 + n) if m < 2 else n) * SHARE
            value = (first if m < 2 else second)[:, at:at + SHARE]
            if n < 2:
                keep_ref[n, m] = value
            else:
                send_ref[n - 2, m] = value.astype(BF)


def main_grads(at, data, cot, parts, act):
    count = EXPERTS * CAP
    block = 512
    return pl.pallas_call(
        grads_kernel,
        grid=(D // block,),
        out_shape=(jax.ShapeDtypeStruct((2, 3, D, SHARE), F32), jax.ShapeDtypeStruct((2, 3, D, SHARE), BF)),
        in_specs=[whole(pltpu.SMEM),
                  pl.BlockSpec((count, block), lambda i: (0, i)),
                  pl.BlockSpec((count, block), lambda i: (0, i)),
                  pl.BlockSpec((2, H // SHARE, count, SHARE), lambda i: (0, 0, 0, 0)),
                  pl.BlockSpec((H // SHARE, count, SHARE), lambda i: (0, 0, 0))],
        out_specs=(pl.BlockSpec((2, 3, block, SHARE), lambda i: (0, 0, i, 0)),
                   pl.BlockSpec((2, 3, block, SHARE), lambda i: (0, 0, i, 0))),
        compiler_params=pltpu.CompilerParams(vmem_limit_bytes=40 * MIB),
        cost_estimate=cost(6 * count * D * H, 12 * MIB),
        name="main_grads",
    )(at, data, cot, parts, act)


def cut_kernel(at_ref, gate_ref, up_ref, down_ref, *out_refs):
    core, xl, y = at_ref[0], at_ref[2], at_ref[3]
    for k, out_ref in enumerate(out_refs):
        lane = pl.multiple_of(((xl + k // NY) & 1) * SHARE, SHARE)
        start = ((y + k % NY) & 3) * (2 * PIECE) + core * PIECE

        def body(z, carry, out_ref=out_ref, lane=lane, start=start):
            at = pl.multiple_of(z * (D // NZ) + start, PIECE)
            for m, ref in enumerate((gate_ref, up_ref, down_ref)):
                out_ref[z, m] = ref[0, pl.ds(at, PIECE), pl.ds(lane, SHARE)]
            return carry

        lax.fori_loop(0, NZ, body, 0)


def cut_weights(at, weights):
    block = (NZ, 3, PIECE, SHARE)
    return pl.pallas_call(
        cut_kernel,
        out_shape=(jax.ShapeDtypeStruct(block, BF),) * 8,
        grid_spec=pltpu.PrefetchScalarGridSpec(
            num_scalar_prefetch=1,
            grid=(1,),
            in_specs=[pl.BlockSpec((1, D, 2 * SHARE), lambda i, s: (0, 0, s[1]))] * 3,
            out_specs=(pl.BlockSpec(block, lambda i, s: (0, 0, 0, 0)),) * 8),
        compiler_params=pltpu.CompilerParams(vmem_limit_bytes=24 * MIB),
        cost_estimate=cost(0, 5 * MIB),
        name="cut_weights",
    )(at, *weights)


def pick_plane_kernel(at_ref, *refs):
    ins, outs = refs[:8], refs[8:]
    z = at_ref[2]
    for m in range(2):
        for k in range(8):
            @pl.when(at_ref[m] == k)
            def _():
                for d in range(NZ):
                    outs[d][m] = ins[k][(z + d) & 7]


def pick_depth_kernel(at_ref, *refs):
    ins, (own_ref, other_ref) = refs[:8], refs[8:]
    core = at_ref[2]
    for d in range(NZ):
        @pl.when(at_ref[0] == d)
        def _():
            own_ref[...] = ins[d][core]

        @pl.when(at_ref[1] == d)
        def _():
            other_ref[...] = ins[d][1 - core]


def place_kernel(at_ref, *refs):
    for d in range(NY):
        refs[NY][(at_ref[0] - d) & 3] = refs[d][...]


def hot_kernel(at_ref, r0, r1, r2, r3, weights_ref, o0, o1, o2, o3, g0, g1, g2, g3, rows_ref, data_ref, cot_ref):
    block = 2 * PAIR
    total = 4 * block
    count = total // 2
    for n, ref in enumerate((r0, r1, r2, r3)):
        rows_ref[n * block:(n + 1) * block, :] = ref[...]

    def place(i):
        group = jnp.floor((i.astype(F32) + 0.5) * (1.0 / HOT_CAP)).astype(jnp.int32)
        return group * HOT_CAP + i

    i, j = iota((count, total), 0), iota((count, total), 1)
    at = place(i)
    data_ref[...] = jnp.dot(onehot(j == at), rows_ref[...], preferred_element_type=F32).astype(BF)
    cot_ref[...] = jnp.dot(onehot(j == at + HOT_CAP), rows_ref[...], preferred_element_type=F32).astype(BF)
    data, cot = data_ref[...], cot_ref[...]
    gate_w, up_w, down_w = (weights_ref[:, m].reshape(D, SHARE) for m in range(3))
    gate = jnp.dot(data, gate_w, preferred_element_type=F32)
    up = jnp.dot(data, up_w, preferred_element_type=F32)
    back = jnp.dot(cot, down_w, preferred_element_type=F32)
    act = (gate * jax.nn.sigmoid(gate) * up).astype(BF)
    gate_part, up_part = backward_parts(gate, up, back)
    out = contract(act, down_w, 1, 1).astype(BF)
    inp = (contract(gate_part, gate_w, 1, 1) + contract(up_part, up_w, 1, 1)).astype(BF)
    i, j = iota((total, count), 1), iota((total, count), 0)
    at = place(i)
    rows_ref[...] = (jnp.dot(onehot(j == at), out, preferred_element_type=F32)
                     + jnp.dot(onehot(j == at + HOT_CAP), inp, preferred_element_type=F32)).astype(BF)
    for n, ref in enumerate((o0, o1, o2, o3)):
        ref[...] = rows_ref[n * block:(n + 1) * block, :]
    width = D // NY
    for d, ref in enumerate((g0, g1, g2, g3)):
        cols = pl.ds(pl.multiple_of(((at_ref[0] + d) & 3) * width, width), width)
        ref[0] = contract(data_ref[:, cols], gate_part, 0, 0).astype(BF)
        ref[1] = contract(data_ref[:, cols], up_part, 0, 0).astype(BF)
        ref[2] = contract(cot_ref[:, cols], act, 0, 0).astype(BF)


def run_hot(at, rows, weights):
    block = 2 * PAIR
    return pl.pallas_call(
        hot_kernel,
        out_shape=(jax.ShapeDtypeStruct((block, D), BF),) * 4 + (jax.ShapeDtypeStruct((3, D // NY, SHARE), BF),) * 4,
        in_specs=[whole(pltpu.SMEM)] + [whole()] * 5,
        out_specs=(whole(),) * 8,
        scratch_shapes=[pltpu.VMEM((4 * block, D), BF), pltpu.VMEM((2 * block, D), BF), pltpu.VMEM((2 * block, D), BF)],
        compiler_params=pltpu.CompilerParams(vmem_limit_bytes=40 * MIB),
        cost_estimate=cost(18 * 96 * D * SHARE, 5 * MIB),
        name="hot",
    )(at, *rows, weights)


def sum_rows_kernel(p0, p1, p2, p3, out_ref):
    out_ref[...] = ((p0[...].astype(F32) + p1[...].astype(F32))
                    + (p2[...].astype(F32) + p3[...].astype(F32))).astype(BF)


def sum_y_kernel(at_ref, p0, p1, p2, p3, *out_refs):
    for d, out_ref in enumerate(out_refs):
        rows = pl.ds(pl.multiple_of(((at_ref[0] + d) & 7) * (2 * PIECE), 2 * PIECE), 2 * PIECE)
        out_ref[...] = ((p0[:, rows, :].astype(F32) + p1[:, rows, :].astype(F32))
                        + (p2[:, rows, :].astype(F32) + p3[:, rows, :].astype(F32))).astype(BF)


def sum_z_kernel(at_ref, *refs):
    ins, (keep_ref, give_ref) = refs[:8], refs[8:]
    core = at_ref[0]
    for ref, half in ((keep_ref, core), (give_ref, 1 - core)):
        rows = pl.ds(pl.multiple_of(half * PIECE, PIECE), PIECE)
        total = ins[0][:, rows, :].astype(F32)
        for part in ins[1:]:
            total = total + part[:, rows, :].astype(F32)
        ref[...] = total.astype(BF)


def combine_kernel(back_ref, input_back_ref, mine_ref, theirs_ref, slots_ref, combine_ref, cot_ref,
                   mixed_ref, input_ref, cgrad_ref):
    slot = [slots_ref[:, k:k + 1] for k in range(2)]

    def pick(base, count, shift):
        lane = iota((TOK, count), 1)
        return [(lane == s + (shift - base)) & (s >= base) for s in slot]

    def both(masks):
        return onehot(masks[0] | masks[1])

    hot = ((mine_ref, SENT), (theirs_ref, SENT + PAIR))
    sums = [0.0, 0.0]
    for h in range(2):
        cols = slice(h * HALF, (h + 1) * HALF)
        main = pick(0, SENT, h * CAP)
        outs = []
        for k in range(2):
            total = jnp.dot(onehot(main[k]), back_ref[...], preferred_element_type=F32)
            for ref, base in hot:
                total = total + jnp.dot(onehot(pick(base, PAIR, 0)[k]), ref[:, cols], preferred_element_type=F32)
            outs.append(total)
        total = 0.0
        for k in range(2):
            total = total + jnp.dot(onehot(main[k]), input_back_ref[...], preferred_element_type=F32)
            for ref, base in hot:
                total = total + jnp.dot(onehot(pick(base, PAIR, HOT_CAP)[k]), ref[:, cols], preferred_element_type=F32)
        input_ref[:, cols] = total.astype(BF)
        mixed_ref[:, cols] = (combine_ref[:, 0:1] * outs[0] + combine_ref[:, 1:2] * outs[1]).astype(BF)
        cot = cot_ref[:, cols].astype(F32)
        for k in range(2):
            sums[k] = sums[k] + jnp.sum(outs[k] * cot, axis=1, keepdims=True)
    for k in range(2):
        cgrad_ref[:, k:k + 1] = sums[k]


def finish_kernel(at_ref, part_ref, other_ref, got_ref, recv_ref, *out_refs):
    core = at_ref[0]

    def body(z, carry):
        for y in range(NY):
            base = y * (D // NY) + z * (2 * PIECE)
            for m in range(3):
                for half, piece in ((core, got_ref[z, core, y, m]), (1 - core, recv_ref[z, y, m])):
                    rows = pl.ds(pl.multiple_of(base + half * PIECE, PIECE), PIECE)
                    out_refs[m][0, rows, :] = (part_ref[m, rows, :] + other_ref[m, rows, :].astype(F32)
                                               + piece.astype(F32))
        return carry

    lax.fori_loop(0, NZ, body, 0)


def exchange(x, axes):
    return lax.all_to_all(x, axes, split_axis=0, concat_axis=0, tiled=True)


def swap(x, axis):
    return lax.ppermute(x, axis, [(0, 1), (1, 0)])


def shift(x, axis, size, d):
    return lax.ppermute(x, axis, [(i, (i + d) % size) for i in range(size)])


def shift_plane(x, k):
    return lax.ppermute(x, S, [(a * NY + b, (a ^ (k // NY)) * NY + (b + k % NY) % NY)
                               for a in range(NXL) for b in range(NY)])


def flip_x(x, m):
    return lax.ppermute(x, X, [(i, i ^ m) for i in range(4)])


def per_device(tokens, cotangent, routes, combine, counts, gate_weight, up_weight, down_weight):
    z, xl, y, xh, core = (lax.axis_index(a) for a in ALL)
    at = scalars(core, xh, xl, y, z)
    weights = (gate_weight, up_weight, down_weight)
    ids = jnp.arange(EXPERTS, dtype=jnp.int32)
    root0 = jnp.argmax(counts).astype(jnp.int32)
    root1 = jnp.argmax(jnp.where(ids == root0, jnp.iinfo(jnp.int32).min, counts)).astype(jnp.int32)
    rz, rxl, ry = zip(*((r // (NXL * NY), (r // NY) % NXL, r % NY) for r in (root0, root1)))

    cut = cut_weights(at, weights)
    data_send, scaled_send, mine, theirs, slots = pack(
        at, counts.reshape(1, EXPERTS), routes.T, combine.T, tokens, cotangent)
    plane = [cut[0]] + [shift_plane(cut[k], k) for k in range(1, 8)]
    data_got = exchange(data_send, E)
    from_plane = [(xl ^ rxl[m]) * NY + ((y - ry[m]) & 3) for m in range(2)]
    depth = call(pick_plane_kernel, "pick_plane", [((2, 3, PIECE, SHARE), BF)] * 8,
                 (scalars(from_plane[0], from_plane[1], z), *plane))
    depth = [depth[0]] + [shift(depth[d], "z", NZ, d) for d in range(1, NZ)]
    scaled_got = exchange(scaled_send, E)
    far = [(z - rz[m]) & 7 for m in range(2)]
    first = core == 0
    own, other = call(pick_depth_kernel, "pick_depth", [((3, PIECE, SHARE), BF)] * 2,
                      (scalars(jnp.where(first, far[0], far[1]), jnp.where(first, far[1], far[0]), core), *depth))
    other = swap(other, "c")
    piece = jnp.where(first, jnp.stack([own, other]), jnp.stack([other, own]))
    pieces = [piece] + [shift(piece, "y", NY, d) for d in range(1, NY)]
    row, = call(place_kernel, "place", [((NY, 2, 3, PIECE, SHARE), BF)], (y.reshape(1), *pieces))
    shared = lax.all_gather(row.reshape(-1, SHARE), "z", axis=0, tiled=True).reshape(EXPERTS, 3, PIECE, SHARE)

    hot_rows = jnp.concatenate([mine, swap(theirs, "c")], axis=0)
    hot_rows = [hot_rows] + [flip_x(hot_rows, m) for m in range(1, 4)]

    out_send, data, gate, up, act = expert_forward(data_got, weights)
    out_back = exchange(out_send, E)
    input_send, cot, parts = expert_backward(scaled_got, gate, up, weights)
    input_back = exchange(input_send, E)

    made = run_hot(y.reshape(1), hot_rows, shared)
    ret = [made[0]] + [flip_x(made[m], m) for m in range(1, 4)]
    hot_back, = call(sum_rows_kernel, "sum_rows", [((2 * PAIR, D), BF)], ret)
    hot_mine = hot_back[:PAIR]
    hot_theirs = swap(hot_back[PAIR:], "c")
    by_y = [made[4]] + [shift(made[4 + d], "y", NY, d) for d in range(1, NY)]
    by_z = call(sum_y_kernel, "sum_y", [((3, 2 * PIECE, SHARE), BF)] * 8, (z.reshape(1), *by_y))
    by_z = [by_z[0]] + [shift(by_z[d], "z", NZ, d) for d in range(1, NZ)]
    own, other = call(sum_z_kernel, "sum_z", [((3, PIECE, SHARE), BF)] * 2, (core.reshape(1), *by_z))
    other = swap(other, "c")
    dest = iota((EXPERTS, 1, 1, 1), 0)
    home = jnp.where(dest == jnp.where(first, root0, root1), own[None],
                     jnp.where(dest == jnp.where(first, root1, root0), other[None], jnp.zeros((), BF)))
    home = exchange(home.reshape(-1, SHARE), E).reshape(NZ, NXL, NY, 3, PIECE, SHARE)
    rest = swap(lax.dynamic_index_in_dim(home, 1 - core, 1, keepdims=False), "c")

    keep, give = main_grads(at, data, cot, parts, act)
    half = keep + swap(give, "c").astype(F32)
    part = lax.dynamic_index_in_dim(half, xh, 0, keepdims=False)
    across = swap(lax.dynamic_index_in_dim(half, 1 - xh, 0, keepdims=False).astype(BF), "xh")

    mixed, input_grad, combine_grad = call(
        combine_kernel, "combine", [((TOK, D), BF), ((TOK, D), BF), ((TOK, 2), F32)],
        (out_back, input_back, hot_mine, hot_theirs, slots.T, combine, cotangent), 6 * TOK * SENT * D, 4 * MIB, 32)
    grads = call(finish_kernel, "finish", [((1, D, SHARE), F32)] * 3,
                 (core.reshape(1), part, across, home, rest), 0, 8 * MIB)
    return mixed, input_grad, combine_grad, *grads


def solution(mesh):
    split = Mesh(mesh.devices.reshape(NZ, NXL, NY, NXH, NC), ALL)
    rows = P(ALL, None)
    owned = P(E, None, None)
    grads = P(E, None, ("xh", "c"))
    return jax.shard_map(
        per_device,
        mesh=split,
        in_specs=(rows, rows, rows, rows, P(), owned, owned, owned),
        out_specs=(rows, rows, rows, grads, grads, grads),
        check_vma=False,
    )
```

```python
import functools

import jax
import jax.numpy as jnp
from jax import lax
from jax.experimental import pallas as pl
from jax.experimental.pallas import tpu as pltpu
from jax.sharding import Mesh
from jax.sharding import PartitionSpec as P

D = 2048
H = 512
TOK = 128
EXPERTS = 64
CAP = 4
HOT_CAP = 12
SLOT = 2 * CAP
SENT = EXPERTS * SLOT
PAIR = 2 * HOT_CAP
SHARE = 128
WROWS = 3 * D
NZ, NXL, NY, NXH, NC = 8, 2, 4, 2, 2
ALL = ("z", "xl", "y", "xh", "c")
E = ("z", "xl", "y")
X = ("xl", "xh")
S = ("xl", "y")
PIECE = 32
BF = jnp.bfloat16
F32 = jnp.float32
MIB = 1024 * 1024


def contract(a, b, da, db):
    return lax.dot_general(a, b, (((da,), (db,)), ((), ())), preferred_element_type=F32)


def iota(shape, dim):
    return lax.broadcasted_iota(jnp.int32, shape, dim)


def cost(flops, nbytes):
    return pl.CostEstimate(flops=int(flops), bytes_accessed=int(nbytes), transcendentals=0)


def block_of(x):
    if x.ndim == 1:
        return pl.BlockSpec(memory_space=pltpu.SMEM)
    return pl.BlockSpec(x.shape, lambda i, n=x.ndim: (0,) * n)


def scalars(*values):
    return jnp.stack([jnp.asarray(v, jnp.int32) for v in values])


def call(kernel, name, out, args, flops=0, moved=2 * MIB, vmem=24, scratch=()):
    outs = tuple(jax.ShapeDtypeStruct(shape, dtype) for shape, dtype in out)
    return pl.pallas_call(
        kernel,
        grid=(1,),
        out_shape=outs,
        in_specs=[block_of(a) for a in args],
        out_specs=tuple(block_of(o) for o in outs),
        scratch_shapes=[pltpu.VMEM(shape, BF) for shape in scratch],
        compiler_params=pltpu.CompilerParams(vmem_limit_bytes=vmem * MIB),
        cost_estimate=cost(flops, moved),
        name=name,
    )(*args)


def onehot(mask):
    return mask.astype(F32).astype(BF)


def pack_kernel(at_ref, counts_ref, routes_ref, combine_ref, tokens_ref, cot_ref,
                send_ref, mine_ref, theirs_ref, slots_ref):
    core = at_ref[0]
    counts = counts_ref[...].astype(F32)
    ids = iota((1, EXPERTS), 1).astype(F32)
    low = jnp.float32(-3.0e38)

    def largest(values):
        top = jnp.max(values, axis=1, keepdims=True)
        return jnp.min(jnp.where(values == top, ids, float(EXPERTS)), axis=1, keepdims=True)

    hot0 = largest(counts)
    hot1 = largest(jnp.where(ids == hot0, low, counts))
    eid = iota((EXPERTS, TOK), 0)
    routes = [routes_ref[k:k + 1, :] for k in range(2)]
    weight = [combine_ref[k:k + 1, :] for k in range(2)]
    oh = [(eid == r).astype(F32) for r in routes]
    earlier = (iota((TOK, TOK), 0) < iota((TOK, TOK), 1)).astype(F32).astype(BF)
    cum = jnp.dot((oh[0] + oh[1]).astype(BF), earlier, preferred_element_type=F32)
    rank = [jnp.sum(cum * oh[0], axis=0, keepdims=True),
            jnp.sum((cum + oh[0]) * oh[1], axis=0, keepdims=True)]
    main, mine, theirs = [], [], []
    for k in range(2):
        rf = routes[k].astype(F32)
        lead = rf == hot0
        hot = lead | (rf == hot1)
        member = jnp.where(lead, 0, 1)
        r = rank[k].astype(jnp.int32)
        keep = r < jnp.where(hot, HOT_CAP, CAP)
        main.append(jnp.where(keep & jnp.logical_not(hot), routes[k] * SLOT + r, -1))
        mine.append(jnp.where(keep & hot & (member == core), r, -1))
        theirs.append(jnp.where(keep & hot & (member != core), r, -1))
        slots_ref[k:k + 1, :] = jnp.where(
            main[k] >= 0, main[k],
            jnp.where(mine[k] >= 0, SENT + mine[k], jnp.where(theirs[k] >= 0, SENT + PAIR + theirs[k], -1)))

    def rows(slot, shift, base, count):
        sid = iota((count, TOK), 0) + base
        at = [jnp.where(s >= 0, s + shift, -1) for s in slot]
        hit = [sid == s for s in slot]
        hit_c = [sid == a for a in at]
        pick = (hit[0] | hit[1]).astype(F32).astype(BF)
        pick_c = (hit_c[0] | hit_c[1]).astype(F32).astype(BF)
        w = jnp.sum(jnp.where(hit_c[0], weight[0], 0.0) + jnp.where(hit_c[1], weight[1], 0.0),
                    axis=1, keepdims=True)
        data = jnp.dot(pick, tokens_ref[...], preferred_element_type=F32)
        cot = jnp.dot(pick_c, cot_ref[...], preferred_element_type=F32)
        return (data + w * cot).astype(BF)

    mine_ref[...] = rows(mine, HOT_CAP, 0, PAIR)
    theirs_ref[...] = rows(theirs, HOT_CAP, 0, PAIR)
    step = 128

    def body(i, carry):
        base = pl.multiple_of(i * step, step)
        send_ref[pl.ds(base, step), :] = rows(main, CAP, base, step)
        return carry

    lax.fori_loop(0, SENT // step, body, 0)


def pack(at, counts, routes_t, combine_t, tokens, cotangent):
    out = [((SENT, D), BF), ((PAIR, D), BF), ((PAIR, D), BF), ((2, TOK), jnp.int32)]
    return call(pack_kernel, "pack", out, (at, counts, routes_t, combine_t, tokens, cotangent),
                4 * SENT * TOK * D, 4 * SENT * D, 32)


def backward_parts(gate, up, back):
    s = jax.nn.sigmoid(gate)
    act = (gate * s * up).astype(BF)
    gate_part = (back * up * s * (1.0 + gate * (1.0 - s))).astype(BF)
    up_part = (back * gate * s).astype(BF)
    return gate_part, up_part, act


def expert_kernel(got_ref, gate_ref, up_ref, down_ref, back_ref, data_ref, cot_ref, parts_ref):
    count = EXPERTS * CAP
    i, j = iota((count, SENT), 0), iota((count, SENT), 1)
    at = (i >> 2) * SLOT + (i & 3)
    data_ref[...] = jnp.dot((j == at).astype(F32).astype(BF), got_ref[...], preferred_element_type=F32).astype(BF)
    cot_ref[...] = jnp.dot((j == at + CAP).astype(F32).astype(BF), got_ref[...], preferred_element_type=F32).astype(BF)
    data, cot = data_ref[...], cot_ref[...]
    gate = jnp.dot(data, gate_ref[0], preferred_element_type=F32)
    up = jnp.dot(data, up_ref[0], preferred_element_type=F32)
    back = jnp.dot(cot, down_ref[0], preferred_element_type=F32)
    gate_part, up_part, act = backward_parts(gate, up, back)
    for m, part in enumerate((gate_part, up_part, act)):
        for q in range(H // SHARE):
            parts_ref[m, q] = part[:, q * SHARE:(q + 1) * SHARE]
    out = contract(act, down_ref[0], 1, 1).astype(BF)
    inp = (contract(gate_part, gate_ref[0], 1, 1) + contract(up_part, up_ref[0], 1, 1)).astype(BF)
    i, j = iota((SENT, count), 1), iota((SENT, count), 0)
    at = (i >> 2) * SLOT + (i & 3)
    back_ref[...] = (jnp.dot((j == at).astype(F32).astype(BF), out, preferred_element_type=F32)
                     + jnp.dot((j == at + CAP).astype(F32).astype(BF), inp, preferred_element_type=F32)).astype(BF)


def run_expert(got, weights):
    count = EXPERTS * CAP
    out = [((SENT, D), BF), ((count, D), BF), ((count, D), BF), ((3, H // SHARE, count, SHARE), BF)]
    return call(expert_kernel, "expert", out, (got,) + weights,
                12 * count * D * H + 8 * SENT * count * D, 12 * MIB, 56)


def grads_kernel(core_ref, data_ref, cot_ref, parts_ref, keep_ref, send_ref):
    core = core_ref[0]
    order = (core, 2 + core, 1 - core, 3 - core)
    pick = [[parts_ref[m, q] for q in order] for m in range(3)]
    first = contract(data_ref[...], jnp.concatenate(pick[0] + pick[1], axis=1), 0, 0)
    second = contract(cot_ref[...], jnp.concatenate(pick[2], axis=1), 0, 0)
    for m in range(3):
        for n in range(4):
            at = ((m * 4 + n) if m < 2 else n) * SHARE
            value = (first if m < 2 else second)[:, at:at + SHARE]
            if n < 2:
                keep_ref[n, m] = value
            else:
                send_ref[n - 2, m] = value.astype(BF)


def main_grads(core, data, cot, parts):
    count = EXPERTS * CAP
    block = 512
    return pl.pallas_call(
        grads_kernel,
        grid=(D // block,),
        out_shape=(jax.ShapeDtypeStruct((2, 3, D, SHARE), F32), jax.ShapeDtypeStruct((2, 3, D, SHARE), BF)),
        in_specs=[pl.BlockSpec(memory_space=pltpu.SMEM),
                  pl.BlockSpec((count, block), lambda i: (0, i)),
                  pl.BlockSpec((count, block), lambda i: (0, i)),
                  pl.BlockSpec((3, H // SHARE, count, SHARE), lambda i: (0, 0, 0, 0))],
        out_specs=(pl.BlockSpec((2, 3, block, SHARE), lambda i: (0, 0, i, 0)),
                   pl.BlockSpec((2, 3, block, SHARE), lambda i: (0, 0, i, 0))),
        compiler_params=pltpu.CompilerParams(vmem_limit_bytes=40 * MIB),
        cost_estimate=cost(6 * count * D * H, 12 * MIB),
        name="main_grads",
    )(core, data, cot, parts)


def cut_kernel(at_ref, gate_ref, up_ref, down_ref, *refs):
    out_refs, turned_ref = refs[:8], refs[8]
    xl, y = at_ref[2], at_ref[3]
    for m, ref in enumerate((gate_ref, up_ref, down_ref)):
        turned_ref[m] = ref[0].T
    for k, out_ref in enumerate(out_refs):
        start = ((xl + k // NY) & 1) * SHARE + ((y + k % NY) & 3) * PIECE
        rows = pl.ds(pl.multiple_of(start, PIECE), PIECE)
        for z in range(NZ):
            for m in range(3):
                out_ref[z, m] = turned_ref[m, rows, z * SHARE:(z + 1) * SHARE]


def cut_weights(at, weights):
    block = (NZ, 3, PIECE, SHARE)
    return pl.pallas_call(
        cut_kernel,
        out_shape=(jax.ShapeDtypeStruct(block, BF),) * 8,
        grid_spec=pltpu.PrefetchScalarGridSpec(
            num_scalar_prefetch=1,
            grid=(1,),
            in_specs=[pl.BlockSpec((1, D // 2, 2 * SHARE), lambda i, s: (0, s[0], s[1]))] * 3,
            out_specs=(pl.BlockSpec(block, lambda i, s: (0, 0, 0, 0)),) * 8,
            scratch_shapes=[pltpu.VMEM((3, 2 * SHARE, D // 2), BF)]),
        compiler_params=pltpu.CompilerParams(vmem_limit_bytes=24 * MIB),
        cost_estimate=cost(0, 5 * MIB),
        name="cut_weights",
    )(at, *weights)


def pick_plane_kernel(at_ref, *refs):
    ins, outs = refs[:8], refs[8:]
    z = at_ref[2]
    for m in range(2):
        for k in range(8):
            @pl.when(at_ref[m] == k)
            def _():
                for d in range(NZ):
                    outs[d][m] = ins[k][(z + d) & 7]


def pick_depth_kernel(at_ref, *refs):
    ins, (own_ref, other_ref) = refs[:8], refs[8:]
    core = at_ref[2]
    for d in range(NZ):
        @pl.when(at_ref[0] == d)
        def _():
            own_ref[...] = ins[d][core]

        @pl.when(at_ref[1] == d)
        def _():
            other_ref[...] = ins[d][1 - core]


def hot_kernel(at_ref, r0, r1, r2, r3, w0, w1, w2, w3, w4, w5, w6, w7, o0, o1, o2, o3, *refs):
    grad_refs, (weights_ref, data_ref, cot_ref, grads_ref) = refs[:8], refs[8:]
    z = at_ref[0]
    for d, ref in enumerate((w0, w1, w2, w3, w4, w5, w6, w7)):
        for half in range(2):
            cols = pl.ds(pl.multiple_of(half * (D // 2) + ((z - d) & 7) * SHARE, SHARE), SHARE)
            for m in range(3):
                weights_ref[m * PIECE:(m + 1) * PIECE, cols] = ref[half, m]
    total = 8 * PAIR
    count = total // 2

    def place(i):
        group = jnp.floor((i.astype(F32) + 0.5) * (1.0 / HOT_CAP)).astype(jnp.int32)
        return group * HOT_CAP + i

    i, j = iota((count, total), 0), iota((count, total), 1)
    at = place(i)
    pick, pick_c = onehot(j == at), onehot(j == at + HOT_CAP)
    for n, ref in enumerate((r0, r1, r2, r3)):
        rows = slice(n * count, (n + 1) * count)
        data_ref[rows, :] = jnp.dot(pick, ref[...], preferred_element_type=F32).astype(BF)
        cot_ref[rows, :] = jnp.dot(pick_c, ref[...], preferred_element_type=F32).astype(BF)
    data, cot = data_ref[...], cot_ref[...]
    both_w, down_w = weights_ref[0:2 * PIECE, :], weights_ref[2 * PIECE:3 * PIECE, :]
    gate = contract(data, weights_ref[0:PIECE, :], 1, 1)
    up = contract(data, weights_ref[PIECE:2 * PIECE, :], 1, 1)
    back = contract(cot, down_w, 1, 1)
    gate_part, up_part, act = backward_parts(gate, up, back)
    both = jnp.concatenate([gate_part, up_part], axis=1)
    out = jnp.dot(act, down_w, preferred_element_type=F32).astype(BF)
    inp = jnp.dot(both, both_w, preferred_element_type=F32).astype(BF)
    grads_ref[0:2 * PIECE, :] = contract(both, data, 0, 0).astype(BF)
    grads_ref[2 * PIECE:3 * PIECE, :] = contract(act, cot, 0, 0).astype(BF)
    width = D // NZ
    for d, ref in enumerate(grad_refs):
        cols = pl.ds(pl.multiple_of(((z + d) & 7) * width, width), width)
        for m in range(3):
            ref[m] = grads_ref[m * PIECE:(m + 1) * PIECE, cols]
    i, j = iota((total, count), 1), iota((total, count), 0)
    at = place(i)
    pick, pick_c = onehot(j == at), onehot(j == at + HOT_CAP)
    for n, ref in enumerate((o0, o1, o2, o3)):
        rows = slice(n * count, (n + 1) * count)
        ref[...] = (jnp.dot(pick, out[rows, :], preferred_element_type=F32)
                    + jnp.dot(pick_c, inp[rows, :], preferred_element_type=F32)).astype(BF)


def run_hot(at, rows, weights):
    total = 8 * PAIR
    out = [((total, D), BF)] * 4 + [((3, PIECE, D // NZ), BF)] * 8
    return call(hot_kernel, "hot", out, (at, *rows, *weights), 72 * total * D * PIECE, 8 * MIB, 48,
                ((3 * PIECE, D), (2 * total, D), (2 * total, D), (3 * PIECE, D)))


def sum_plane_kernel(p0, p1, p2, p3, *out_refs):
    size = 2 * PAIR
    for n, out_ref in enumerate(out_refs):
        rows = slice(n * size, (n + 1) * size)
        out_ref[...] = ((p0[rows, :].astype(F32) + p1[rows, :].astype(F32))
                        + (p2[rows, :].astype(F32) + p3[rows, :].astype(F32))).astype(BF)


def sum_rows_kernel(p0, p1, p2, p3, out_ref):
    out_ref[...] = ((p0[...].astype(F32) + p1[...].astype(F32))
                    + (p2[...].astype(F32) + p3[...].astype(F32))).astype(BF)


def sum_z_kernel(at_ref, *refs):
    ins, (keep_ref, give_ref) = refs[:8], refs[8:]
    core = at_ref[0]
    for ref, half in ((keep_ref, core), (give_ref, 1 - core)):
        cols = pl.ds(pl.multiple_of(half * SHARE, SHARE), SHARE)
        total = ins[0][:, :, cols].astype(F32)
        for part in ins[1:]:
            total = total + part[:, :, cols].astype(F32)
        ref[...] = total.astype(BF)


def combine_kernel(back_ref, mine_ref, theirs_ref, slots_ref, combine_ref, cot_ref,
                   mixed_ref, input_ref, cgrad_ref):
    slot = [slots_ref[:, k:k + 1] for k in range(2)]

    def pick(base, count, shift):
        lane = iota((TOK, count), 1) + (base - shift)
        inside = iota((TOK, count), 1) >= shift
        return [jnp.where((lane == s) & (s >= base) & inside, 1.0, 0.0) for s in slot]

    tables = ((back_ref, 0, SENT, CAP), (mine_ref, SENT, PAIR, HOT_CAP), (theirs_ref, SENT + PAIR, PAIR, HOT_CAP))
    outs = []
    for k in range(2):
        total = None
        for ref, base, count, shift in tables:
            term = jnp.dot(pick(base, count, 0)[k].astype(BF), ref[...], preferred_element_type=F32)
            total = term if total is None else total + term
        outs.append(total)
    total = None
    for ref, base, count, shift in tables:
        both = pick(base, count, shift)
        term = jnp.dot((both[0] + both[1]).astype(BF), ref[...], preferred_element_type=F32)
        total = term if total is None else total + term
    input_ref[...] = total.astype(BF)
    mixed_ref[...] = (combine_ref[:, 0:1] * outs[0] + combine_ref[:, 1:2] * outs[1]).astype(BF)
    cot = cot_ref[...].astype(F32)
    for k in range(2):
        cgrad_ref[:, k:k + 1] = jnp.sum(outs[k] * cot, axis=1, keepdims=True)


def finish_kernel(at_ref, part_ref, other_ref, got_ref, recv_ref, *out_refs):
    core = at_ref[0]
    eye = onehot(iota((SHARE, SHARE), 0) == iota((SHARE, SHARE), 1))

    def body(z, carry):
        for half in range(2):
            rows = pl.ds(pl.multiple_of(z * (2 * SHARE) + (core if half == 0 else 1 - core) * SHARE, SHARE), SHARE)
            for m in range(3):
                piece = jnp.concatenate(
                    [got_ref[z, core, y, m] if half == 0 else recv_ref[z, y, m] for y in range(NY)], axis=0)
                out_refs[m][0, rows, :] = (part_ref[m, rows, :] + other_ref[m, rows, :].astype(F32)
                                           + contract(eye, piece, 1, 1))
        return carry

    lax.fori_loop(0, NZ, body, 0)


def exchange(x, axes):
    return lax.all_to_all(x, axes, split_axis=0, concat_axis=0, tiled=True)


def swap(x, axis):
    return lax.ppermute(x, axis, [(0, 1), (1, 0)])


def shift(x, axis, size, d):
    return lax.ppermute(x, axis, [(i, (i + d) % size) for i in range(size)])


def shift_plane(x, k):
    return lax.ppermute(x, S, [(a * NY + b, (a ^ (k // NY)) * NY + (b + k % NY) % NY)
                               for a in range(NXL) for b in range(NY)])


def flip_x(x, m):
    return lax.ppermute(x, X, [(i, i ^ m) for i in range(4)])


def per_device(tokens, cotangent, routes, combine, counts, gate_weight, up_weight, down_weight):
    z, xl, y, xh, core = (lax.axis_index(a) for a in ALL)
    at = scalars(core, xh, xl, y, z)
    weights = (gate_weight, up_weight, down_weight)
    ids = jnp.arange(EXPERTS, dtype=jnp.int32)
    root0 = jnp.argmax(counts).astype(jnp.int32)
    root1 = jnp.argmax(jnp.where(ids == root0, jnp.iinfo(jnp.int32).min, counts)).astype(jnp.int32)
    rz, rxl, ry = zip(*((r // (NXL * NY), (r // NY) % NXL, r % NY) for r in (root0, root1)))
    first = core == 0

    send, mine, theirs, slots = pack(at, counts.reshape(1, EXPERTS), routes.T, combine.T, tokens, cotangent)
    got = exchange(send, E)

    cut = cut_weights(at, weights)
    plane = [cut[0]] + [shift_plane(cut[k], k) for k in range(1, 8)]
    from_plane = [(xl ^ rxl[m]) * NY + ((y - ry[m]) & 3) for m in range(2)]
    depth = call(pick_plane_kernel, "pick_plane", [((2, 3, PIECE, SHARE), BF)] * 8,
                 (scalars(from_plane[0], from_plane[1], z), *plane))
    depth = [depth[0]] + [shift(depth[d], "z", NZ, d) for d in range(1, NZ)]

    hot_rows = jnp.concatenate([mine, swap(theirs, "c")], axis=0)
    hot_rows = jnp.concatenate([hot_rows] + [flip_x(hot_rows, m) for m in range(1, 4)], axis=0)
    hot_rows = [hot_rows] + [shift(hot_rows, "y", NY, d) for d in range(1, NY)]

    far = [(z - rz[m]) & 7 for m in range(2)]
    own, other = call(pick_depth_kernel, "pick_depth", [((3, PIECE, SHARE), BF)] * 2,
                      (scalars(jnp.where(first, far[0], far[1]), jnp.where(first, far[1], far[0]), core), *depth))
    other = swap(other, "c")
    piece = jnp.where(first, jnp.stack([own, other]), jnp.stack([other, own]))
    piece, got = lax.optimization_barrier((piece, got))
    pieces = [piece] + [shift(piece, "z", NZ, d) for d in range(1, NZ)]

    back, data, cot, parts = run_expert(got, weights)
    back = exchange(back, E)

    made = run_hot(z.reshape(1), hot_rows, pieces)
    by_z = [made[4]] + [shift(made[4 + d], "z", NZ, d) for d in range(1, NZ)]
    by_y = [made[0]] + [shift(made[d], "y", NY, NY - d) for d in range(1, NY)]
    ret = call(sum_plane_kernel, "sum_plane", [((2 * PAIR, D), BF)] * 4, by_y)
    ret = [ret[0]] + [flip_x(ret[m], m) for m in range(1, 4)]
    hot_back, = call(sum_rows_kernel, "sum_rows", [((2 * PAIR, D), BF)], ret)
    hot_mine = hot_back[:PAIR]
    hot_theirs = swap(hot_back[PAIR:], "c")

    keep, give = main_grads(at, data, cot, parts)
    half = keep + swap(give, "c").astype(F32)
    part = lax.dynamic_index_in_dim(half, xh, 0, keepdims=False)
    across = swap(lax.dynamic_index_in_dim(half, 1 - xh, 0, keepdims=False).astype(BF), "xh")

    own, other = call(sum_z_kernel, "sum_z", [((3, PIECE, SHARE), BF)] * 2, (core.reshape(1), *by_z))
    other = swap(other, "c")
    dest = iota((EXPERTS, 1, 1, 1), 0)
    home = jnp.where(dest == jnp.where(first, root0, root1), own[None],
                     jnp.where(dest == jnp.where(first, root1, root0), other[None], jnp.zeros((), BF)))
    home, back = lax.optimization_barrier((home, back))
    home = exchange(home.reshape(-1, SHARE), E).reshape(NZ, NXL, NY, 3, PIECE, SHARE)
    rest = swap(lax.dynamic_index_in_dim(home, 1 - core, 1, keepdims=False), "c")

    mixed, input_grad, combine_grad = call(
        combine_kernel, "combine", [((TOK, D), BF), ((TOK, D), BF), ((TOK, 2), F32)],
        (back, hot_mine, hot_theirs, slots.T, combine, cotangent), 6 * TOK * SENT * D, 4 * MIB, 32)
    grads = call(finish_kernel, "finish", [((1, D, SHARE), F32)] * 3,
                 (core.reshape(1), part, across, home, rest), 0, 8 * MIB, 40)
    return mixed, input_grad, combine_grad, *grads


def solution(mesh):
    split = Mesh(mesh.devices.reshape(NZ, NXL, NY, NXH, NC), ALL)
    rows = P(ALL, None)
    owned = P(E, None, None)
    grads = P(E, None, ("xh", "c"))
    return jax.shard_map(
        per_device,
        mesh=split,
        in_specs=(rows, rows, rows, rows, P(), owned, owned, owned),
        out_specs=(rows, rows, rows, grads, grads, grads),
        check_vma=False,
    )
```

```python
import functools

import jax
import jax.numpy as jnp
from jax import lax
from jax.experimental import pallas as pl
from jax.experimental.pallas import tpu as pltpu
from jax.sharding import Mesh
from jax.sharding import PartitionSpec as P

D = 2048
H = 512
TOK = 128
EXPERTS = 64
CAP = 4
HOT_CAP = 12
SLOT = 2 * CAP
SENT = EXPERTS * SLOT
PAIR = 2 * HOT_CAP
SHARE = 128
WROWS = 3 * D
NZ, NXL, NY, NXH, NC = 8, 2, 4, 2, 2
ALL = ("z", "xl", "y", "xh", "c")
E = ("z", "xl", "y")
X = ("xl", "xh")
S = ("xl", "y")
PIECE = 32
BF = jnp.bfloat16
F32 = jnp.float32
MIB = 1024 * 1024


def contract(a, b, da, db):
    return lax.dot_general(a, b, (((da,), (db,)), ((), ())), preferred_element_type=F32)


def iota(shape, dim):
    return lax.broadcasted_iota(jnp.int32, shape, dim)


def cost(flops, nbytes):
    return pl.CostEstimate(flops=int(flops), bytes_accessed=int(nbytes), transcendentals=0)


def block_of(x):
    if x.ndim == 1:
        return pl.BlockSpec(memory_space=pltpu.SMEM)
    return pl.BlockSpec(x.shape, lambda i, n=x.ndim: (0,) * n)


def scalars(*values):
    return jnp.stack([jnp.asarray(v, jnp.int32) for v in values])


def call(kernel, name, out, args, flops=0, moved=2 * MIB, vmem=24, scratch=()):
    outs = tuple(jax.ShapeDtypeStruct(shape, dtype) for shape, dtype in out)
    return pl.pallas_call(
        kernel,
        grid=(1,),
        out_shape=outs,
        in_specs=[block_of(a) for a in args],
        out_specs=tuple(block_of(o) for o in outs),
        scratch_shapes=[pltpu.VMEM(shape, BF) for shape in scratch],
        compiler_params=pltpu.CompilerParams(vmem_limit_bytes=vmem * MIB),
        cost_estimate=cost(flops, moved),
        name=name,
    )(*args)


def onehot(mask):
    return mask.astype(F32).astype(BF)


def pack_kernel(at_ref, counts_ref, routes_ref, combine_ref, tokens_ref, cot_ref,
                send_ref, mine_ref, theirs_ref, slots_ref):
    core = at_ref[0]
    counts = counts_ref[...].astype(F32)
    ids = iota((1, EXPERTS), 1).astype(F32)
    low = jnp.float32(-3.0e38)

    def largest(values):
        top = jnp.max(values, axis=1, keepdims=True)
        return jnp.min(jnp.where(values == top, ids, float(EXPERTS)), axis=1, keepdims=True)

    hot0 = largest(counts)
    hot1 = largest(jnp.where(ids == hot0, low, counts))
    eid = iota((EXPERTS, TOK), 0)
    routes = [routes_ref[k:k + 1, :] for k in range(2)]
    weight = [combine_ref[k:k + 1, :] for k in range(2)]
    oh = [(eid == r).astype(F32) for r in routes]
    earlier = (iota((TOK, TOK), 0) < iota((TOK, TOK), 1)).astype(F32).astype(BF)
    cum = jnp.dot((oh[0] + oh[1]).astype(BF), earlier, preferred_element_type=F32)
    rank = [jnp.sum(cum * oh[0], axis=0, keepdims=True),
            jnp.sum((cum + oh[0]) * oh[1], axis=0, keepdims=True)]
    main, mine, theirs = [], [], []
    for k in range(2):
        rf = routes[k].astype(F32)
        lead = rf == hot0
        hot = lead | (rf == hot1)
        member = jnp.where(lead, 0, 1)
        r = rank[k].astype(jnp.int32)
        keep = r < jnp.where(hot, HOT_CAP, CAP)
        main.append(jnp.where(keep & jnp.logical_not(hot), routes[k] * SLOT + r, -1))
        mine.append(jnp.where(keep & hot & (member == core), r, -1))
        theirs.append(jnp.where(keep & hot & (member != core), r, -1))
        slots_ref[k:k + 1, :] = jnp.where(
            main[k] >= 0, main[k],
            jnp.where(mine[k] >= 0, SENT + mine[k], jnp.where(theirs[k] >= 0, SENT + PAIR + theirs[k], -1)))

    def rows(slot, shift, base, count):
        sid = iota((count, TOK), 0) + base
        at = [jnp.where(s >= 0, s + shift, -1) for s in slot]
        hit = [sid == s for s in slot]
        hit_c = [sid == a for a in at]
        pick = (hit[0] | hit[1]).astype(F32).astype(BF)
        pick_c = (hit_c[0] | hit_c[1]).astype(F32).astype(BF)
        w = jnp.sum(jnp.where(hit_c[0], weight[0], 0.0) + jnp.where(hit_c[1], weight[1], 0.0),
                    axis=1, keepdims=True)
        data = jnp.dot(pick, tokens_ref[...], preferred_element_type=F32)
        cot = jnp.dot(pick_c, cot_ref[...], preferred_element_type=F32)
        return (data + w * cot).astype(BF)

    mine_ref[...] = rows(mine, HOT_CAP, 0, PAIR)
    theirs_ref[...] = rows(theirs, HOT_CAP, 0, PAIR)
    step = 128

    def body(i, carry):
        base = pl.multiple_of(i * step, step)
        send_ref[pl.ds(base, step), :] = rows(main, CAP, base, step)
        return carry

    lax.fori_loop(0, SENT // step, body, 0)


def pack(at, counts, routes_t, combine_t, tokens, cotangent):
    out = [((SENT, D), BF), ((PAIR, D), BF), ((PAIR, D), BF), ((2, TOK), jnp.int32)]
    return call(pack_kernel, "pack", out, (at, counts, routes_t, combine_t, tokens, cotangent),
                4 * SENT * TOK * D, 4 * SENT * D, 32)


def backward_parts(gate, up, back):
    s = jax.nn.sigmoid(gate)
    act = (gate * s * up).astype(BF)
    gate_part = (back * up * s * (1.0 + gate * (1.0 - s))).astype(BF)
    up_part = (back * gate * s).astype(BF)
    return gate_part, up_part, act


def expert_kernel(got_ref, gate_ref, up_ref, down_ref, back_ref, data_ref, cot_ref, parts_ref):
    count = EXPERTS * CAP
    i, j = iota((count, SENT), 0), iota((count, SENT), 1)
    at = (i >> 2) * SLOT + (i & 3)
    data_ref[...] = jnp.dot((j == at).astype(F32).astype(BF), got_ref[...], preferred_element_type=F32).astype(BF)
    cot_ref[...] = jnp.dot((j == at + CAP).astype(F32).astype(BF), got_ref[...], preferred_element_type=F32).astype(BF)
    data, cot = data_ref[...], cot_ref[...]
    gate = jnp.dot(data, gate_ref[0], preferred_element_type=F32)
    up = jnp.dot(data, up_ref[0], preferred_element_type=F32)
    back = jnp.dot(cot, down_ref[0], preferred_element_type=F32)
    gate_part, up_part, act = backward_parts(gate, up, back)
    for m, part in enumerate((gate_part, up_part, act)):
        for q in range(H // SHARE):
            parts_ref[m, q] = part[:, q * SHARE:(q + 1) * SHARE]
    out = contract(act, down_ref[0], 1, 1).astype(BF)
    inp = (contract(gate_part, gate_ref[0], 1, 1) + contract(up_part, up_ref[0], 1, 1)).astype(BF)
    i, j = iota((SENT, count), 1), iota((SENT, count), 0)
    at = (i >> 2) * SLOT + (i & 3)
    back_ref[...] = (jnp.dot((j == at).astype(F32).astype(BF), out, preferred_element_type=F32)
                     + jnp.dot((j == at + CAP).astype(F32).astype(BF), inp, preferred_element_type=F32)).astype(BF)


def run_expert(got, weights):
    count = EXPERTS * CAP
    out = [((SENT, D), BF), ((count, D), BF), ((count, D), BF), ((3, H // SHARE, count, SHARE), BF)]
    return call(expert_kernel, "expert", out, (got,) + weights,
                12 * count * D * H + 8 * SENT * count * D, 12 * MIB, 56)


def grads_kernel(core_ref, data_ref, cot_ref, parts_ref, keep_ref, send_ref):
    core = core_ref[0]
    order = (core, 2 + core, 1 - core, 3 - core)
    pick = [[parts_ref[m, q] for q in order] for m in range(3)]
    first = contract(data_ref[...], jnp.concatenate(pick[0] + pick[1], axis=1), 0, 0)
    second = contract(cot_ref[...], jnp.concatenate(pick[2], axis=1), 0, 0)
    for m in range(3):
        for n in range(4):
            at = ((m * 4 + n) if m < 2 else n) * SHARE
            value = (first if m < 2 else second)[:, at:at + SHARE]
            if n < 2:
                keep_ref[n, m] = value
            else:
                send_ref[n - 2, m] = value.astype(BF)


def main_grads(core, data, cot, parts):
    count = EXPERTS * CAP
    block = 512
    return pl.pallas_call(
        grads_kernel,
        grid=(D // block,),
        out_shape=(jax.ShapeDtypeStruct((2, 3, D, SHARE), F32), jax.ShapeDtypeStruct((2, 3, D, SHARE), BF)),
        in_specs=[pl.BlockSpec(memory_space=pltpu.SMEM),
                  pl.BlockSpec((count, block), lambda i: (0, i)),
                  pl.BlockSpec((count, block), lambda i: (0, i)),
                  pl.BlockSpec((3, H // SHARE, count, SHARE), lambda i: (0, 0, 0, 0))],
        out_specs=(pl.BlockSpec((2, 3, block, SHARE), lambda i: (0, 0, i, 0)),
                   pl.BlockSpec((2, 3, block, SHARE), lambda i: (0, 0, i, 0))),
        compiler_params=pltpu.CompilerParams(vmem_limit_bytes=40 * MIB),
        cost_estimate=cost(6 * count * D * H, 12 * MIB),
        name="main_grads",
    )(core, data, cot, parts)


def cut_kernel(at_ref, gate_ref, up_ref, down_ref, *refs):
    out_refs, turned_ref = refs[:8], refs[8]
    xl, y = at_ref[2], at_ref[3]
    for m, ref in enumerate((gate_ref, up_ref, down_ref)):
        turned_ref[m] = ref[0].T
    for k, out_ref in enumerate(out_refs):
        start = ((xl + k // NY) & 1) * SHARE + ((y + k % NY) & 3) * PIECE
        rows = pl.ds(pl.multiple_of(start, PIECE), PIECE)
        for z in range(NZ):
            for m in range(3):
                out_ref[z, m] = turned_ref[m, rows, z * SHARE:(z + 1) * SHARE]


def cut_weights(at, weights):
    block = (NZ, 3, PIECE, SHARE)
    return pl.pallas_call(
        cut_kernel,
        out_shape=(jax.ShapeDtypeStruct(block, BF),) * 8,
        grid_spec=pltpu.PrefetchScalarGridSpec(
            num_scalar_prefetch=1,
            grid=(1,),
            in_specs=[pl.BlockSpec((1, D // 2, 2 * SHARE), lambda i, s: (0, s[0], s[1]))] * 3,
            out_specs=(pl.BlockSpec(block, lambda i, s: (0, 0, 0, 0)),) * 8,
            scratch_shapes=[pltpu.VMEM((3, 2 * SHARE, D // 2), BF)]),
        compiler_params=pltpu.CompilerParams(vmem_limit_bytes=24 * MIB),
        cost_estimate=cost(0, 5 * MIB),
        name="cut_weights",
    )(at, *weights)


def pick_plane_kernel(at_ref, *refs):
    ins, outs = refs[:8], refs[8:]
    z = at_ref[2]
    for m in range(2):
        for k in range(8):
            @pl.when(at_ref[m] == k)
            def _():
                for d in range(NZ):
                    outs[d][m] = ins[k][(z + d) & 7]


def pick_depth_kernel(at_ref, *refs):
    ins, (own_ref, other_ref) = refs[:8], refs[8:]
    core = at_ref[2]
    for d in range(NZ):
        @pl.when(at_ref[0] == d)
        def _():
            own_ref[...] = ins[d][core]

        @pl.when(at_ref[1] == d)
        def _():
            other_ref[...] = ins[d][1 - core]


def hot_kernel(at_ref, r0, r1, r2, r3, w0, w1, w2, w3, w4, w5, w6, w7, o0, o1, o2, o3, *refs):
    grad_refs, (weights_ref, data_ref, cot_ref, grads_ref) = refs[:8], refs[8:]
    z = at_ref[0]
    for d, ref in enumerate((w0, w1, w2, w3, w4, w5, w6, w7)):
        for half in range(2):
            cols = pl.ds(pl.multiple_of(half * (D // 2) + ((z - d) & 7) * SHARE, SHARE), SHARE)
            for m in range(3):
                weights_ref[m * PIECE:(m + 1) * PIECE, cols] = ref[half, m]
    total = 8 * PAIR
    count = total // 2

    def place(i):
        group = jnp.floor((i.astype(F32) + 0.5) * (1.0 / HOT_CAP)).astype(jnp.int32)
        return group * HOT_CAP + i

    i, j = iota((count, total), 0), iota((count, total), 1)
    at = place(i)
    pick, pick_c = onehot(j == at), onehot(j == at + HOT_CAP)
    for n, ref in enumerate((r0, r1, r2, r3)):
        rows = slice(n * count, (n + 1) * count)
        data_ref[rows, :] = jnp.dot(pick, ref[...], preferred_element_type=F32).astype(BF)
        cot_ref[rows, :] = jnp.dot(pick_c, ref[...], preferred_element_type=F32).astype(BF)
    data, cot = data_ref[...], cot_ref[...]
    both_w, down_w = weights_ref[0:2 * PIECE, :], weights_ref[2 * PIECE:3 * PIECE, :]
    gate = contract(data, weights_ref[0:PIECE, :], 1, 1)
    up = contract(data, weights_ref[PIECE:2 * PIECE, :], 1, 1)
    back = contract(cot, down_w, 1, 1)
    gate_part, up_part, act = backward_parts(gate, up, back)
    both = jnp.concatenate([gate_part, up_part], axis=1)
    out = jnp.dot(act, down_w, preferred_element_type=F32).astype(BF)
    inp = jnp.dot(both, both_w, preferred_element_type=F32).astype(BF)
    grads_ref[0:2 * PIECE, :] = contract(both, data, 0, 0).astype(BF)
    grads_ref[2 * PIECE:3 * PIECE, :] = contract(act, cot, 0, 0).astype(BF)
    width = D // NZ
    for d, ref in enumerate(grad_refs):
        cols = pl.ds(pl.multiple_of(((z + d) & 7) * width, width), width)
        for m in range(3):
            ref[m] = grads_ref[m * PIECE:(m + 1) * PIECE, cols]
    i, j = iota((total, count), 1), iota((total, count), 0)
    at = place(i)
    pick, pick_c = onehot(j == at), onehot(j == at + HOT_CAP)
    for n, ref in enumerate((o0, o1, o2, o3)):
        rows = slice(n * count, (n + 1) * count)
        ref[...] = (jnp.dot(pick, out[rows, :], preferred_element_type=F32)
                    + jnp.dot(pick_c, inp[rows, :], preferred_element_type=F32)).astype(BF)


def run_hot(at, rows, weights):
    total = 8 * PAIR
    out = [((total, D), BF)] * 4 + [((3, PIECE, D // NZ), BF)] * 8
    return call(hot_kernel, "hot", out, (at, *rows, *weights), 72 * total * D * PIECE, 8 * MIB, 48,
                ((3 * PIECE, D), (2 * total, D), (2 * total, D), (3 * PIECE, D)))


def sum_plane_kernel(p0, p1, p2, p3, *out_refs):
    size = 2 * PAIR
    for n, out_ref in enumerate(out_refs):
        rows = slice(n * size, (n + 1) * size)
        out_ref[...] = ((p0[rows, :].astype(F32) + p1[rows, :].astype(F32))
                        + (p2[rows, :].astype(F32) + p3[rows, :].astype(F32))).astype(BF)


def sum_rows_kernel(p0, p1, p2, p3, out_ref):
    out_ref[...] = ((p0[...].astype(F32) + p1[...].astype(F32))
                    + (p2[...].astype(F32) + p3[...].astype(F32))).astype(BF)


def sum_z_kernel(at_ref, *refs):
    ins, (keep_ref, give_ref) = refs[:8], refs[8:]
    core = at_ref[0]
    for ref, half in ((keep_ref, core), (give_ref, 1 - core)):
        cols = pl.ds(pl.multiple_of(half * SHARE, SHARE), SHARE)
        total = ins[0][:, :, cols].astype(F32)
        for part in ins[1:]:
            total = total + part[:, :, cols].astype(F32)
        ref[...] = total.astype(BF)


def combine_kernel(back_ref, mine_ref, theirs_ref, slots_ref, combine_ref, cot_ref,
                   mixed_ref, input_ref, cgrad_ref):
    slot = [slots_ref[:, k:k + 1] for k in range(2)]

    def pick(base, count, shift):
        lane = iota((TOK, count), 1) + (base - shift)
        inside = iota((TOK, count), 1) >= shift
        return [jnp.where((lane == s) & (s >= base) & inside, 1.0, 0.0) for s in slot]

    tables = ((back_ref, 0, SENT, CAP), (mine_ref, SENT, PAIR, HOT_CAP), (theirs_ref, SENT + PAIR, PAIR, HOT_CAP))
    outs = []
    for k in range(2):
        total = None
        for ref, base, count, shift in tables:
            term = jnp.dot(pick(base, count, 0)[k].astype(BF), ref[...], preferred_element_type=F32)
            total = term if total is None else total + term
        outs.append(total)
    total = None
    for ref, base, count, shift in tables:
        both = pick(base, count, shift)
        term = jnp.dot((both[0] + both[1]).astype(BF), ref[...], preferred_element_type=F32)
        total = term if total is None else total + term
    input_ref[...] = total.astype(BF)
    mixed_ref[...] = (combine_ref[:, 0:1] * outs[0] + combine_ref[:, 1:2] * outs[1]).astype(BF)
    cot = cot_ref[...].astype(F32)
    for k in range(2):
        cgrad_ref[:, k:k + 1] = jnp.sum(outs[k] * cot, axis=1, keepdims=True)


def finish_kernel(at_ref, part_ref, other_ref, got_ref, recv_ref, *out_refs):
    core = at_ref[0]
    eye = onehot(iota((SHARE, SHARE), 0) == iota((SHARE, SHARE), 1))
    for half in range(2):
        rows = pl.ds(pl.multiple_of((core if half == 0 else 1 - core) * SHARE, SHARE), SHARE)
        for m in range(3):
            piece = jnp.concatenate(
                [got_ref[0, 0, y, m] if half == 0 else recv_ref[0, y, m] for y in range(NY)], axis=0)
            out_refs[m][0, rows, :] = (part_ref[0, m, rows, :] + other_ref[m, rows, :].astype(F32)
                                       + contract(eye, piece, 1, 1))


def finish(at, half, across, home, rest):
    block = 2 * SHARE
    return pl.pallas_call(
        finish_kernel,
        out_shape=(jax.ShapeDtypeStruct((1, D, SHARE), F32),) * 3,
        grid_spec=pltpu.PrefetchScalarGridSpec(
            num_scalar_prefetch=1,
            grid=(NZ,),
            in_specs=[pl.BlockSpec((1, 3, block, SHARE), lambda i, s: (s[1], 0, i, 0)),
                      pl.BlockSpec((3, block, SHARE), lambda i, s: (0, i, 0)),
                      pl.BlockSpec((1, 1, NY, 3, PIECE, SHARE), lambda i, s: (i, s[0], 0, 0, 0, 0)),
                      pl.BlockSpec((1, NY, 3, PIECE, SHARE), lambda i, s: (i, 0, 0, 0, 0))],
            out_specs=(pl.BlockSpec((1, block, SHARE), lambda i, s: (0, i, 0)),) * 3),
        compiler_params=pltpu.CompilerParams(vmem_limit_bytes=24 * MIB),
        cost_estimate=cost(0, 10 * MIB),
        name="finish",
    )(at, half, across, home, rest)


def exchange(x, axes):
    return lax.all_to_all(x, axes, split_axis=0, concat_axis=0, tiled=True)


def swap(x, axis):
    return lax.ppermute(x, axis, [(0, 1), (1, 0)])


def shift(x, axis, size, d):
    return lax.ppermute(x, axis, [(i, (i + d) % size) for i in range(size)])


def shift_plane(x, k):
    return lax.ppermute(x, S, [(a * NY + b, (a ^ (k // NY)) * NY + (b + k % NY) % NY)
                               for a in range(NXL) for b in range(NY)])


def flip_x(x, m):
    return lax.ppermute(x, X, [(i, i ^ m) for i in range(4)])


def per_device(tokens, cotangent, routes, combine, counts, gate_weight, up_weight, down_weight):
    z, xl, y, xh, core = (lax.axis_index(a) for a in ALL)
    at = scalars(core, xh, xl, y, z)
    weights = (gate_weight, up_weight, down_weight)
    ids = jnp.arange(EXPERTS, dtype=jnp.int32)
    root0 = jnp.argmax(counts).astype(jnp.int32)
    root1 = jnp.argmax(jnp.where(ids == root0, jnp.iinfo(jnp.int32).min, counts)).astype(jnp.int32)
    rz, rxl, ry = zip(*((r // (NXL * NY), (r // NY) % NXL, r % NY) for r in (root0, root1)))
    first = core == 0

    send, mine, theirs, slots = pack(at, counts.reshape(1, EXPERTS), routes.T, combine.T, tokens, cotangent)
    got = exchange(send, E)

    cut = cut_weights(at, weights)
    plane = [cut[0]] + [shift_plane(cut[k], k) for k in range(1, 8)]
    from_plane = [(xl ^ rxl[m]) * NY + ((y - ry[m]) & 3) for m in range(2)]
    ring = jnp.concatenate([mine, swap(theirs, "c")], axis=0)
    ring = jnp.concatenate([ring] + [flip_x(ring, m) for m in range(1, 4)], axis=0)
    plane, ring = lax.optimization_barrier((plane, ring))
    depth = call(pick_plane_kernel, "pick_plane", [((2, 3, PIECE, SHARE), BF)] * 8,
                 (scalars(from_plane[0], from_plane[1], z), *plane))
    depth = [depth[0]] + [shift(depth[d], "z", NZ, d) for d in range(1, NZ)]

    hot_rows = [ring] + [shift(ring, "y", NY, d) for d in range(1, NY)]

    far = [(z - rz[m]) & 7 for m in range(2)]
    own, other = call(pick_depth_kernel, "pick_depth", [((3, PIECE, SHARE), BF)] * 2,
                      (scalars(jnp.where(first, far[0], far[1]), jnp.where(first, far[1], far[0]), core), *depth))
    other = swap(other, "c")
    piece = jnp.where(first, jnp.stack([own, other]), jnp.stack([other, own]))
    piece, hot_rows, got = lax.optimization_barrier((piece, hot_rows, got))
    pieces = [piece] + [shift(piece, "z", NZ, d) for d in range(1, NZ)]

    back, data, cot, parts = run_expert(got, weights)
    back, pieces = lax.optimization_barrier((back, pieces))
    back = exchange(back, E)

    made = run_hot(z.reshape(1), hot_rows, pieces)
    (data, cot, parts), made = lax.optimization_barrier(((data, cot, parts), made))
    by_z = [made[4]] + [shift(made[4 + d], "z", NZ, d) for d in range(1, NZ)]
    by_y = [made[0]] + [shift(made[d], "y", NY, NY - d) for d in range(1, NY)]
    ret = call(sum_plane_kernel, "sum_plane", [((2 * PAIR, D), BF)] * 4, by_y)
    by_z, ret = lax.optimization_barrier((by_z, ret))
    ret = [ret[0]] + [flip_x(ret[m], m) for m in range(1, 4)]
    hot_back, = call(sum_rows_kernel, "sum_rows", [((2 * PAIR, D), BF)], ret)
    hot_mine = hot_back[:PAIR]
    hot_theirs = swap(hot_back[PAIR:], "c")

    keep, give = main_grads(at, data, cot, parts)
    half = keep + swap(give, "c").astype(F32)
    across = swap(lax.dynamic_index_in_dim(half, 1 - xh, 0, keepdims=False).astype(BF), "xh")

    own, other = call(sum_z_kernel, "sum_z", [((3, PIECE, SHARE), BF)] * 2, (core.reshape(1), *by_z))
    other = swap(other, "c")
    dest = iota((EXPERTS, 1, 1, 1), 0)
    home = jnp.where(dest == jnp.where(first, root0, root1), own[None],
                     jnp.where(dest == jnp.where(first, root1, root0), other[None], jnp.zeros((), BF)))
    home, back = lax.optimization_barrier((home, back))
    home = exchange(home.reshape(-1, SHARE), E).reshape(NZ, NXL, NY, 3, PIECE, SHARE)

    mixed, input_grad, combine_grad = call(
        combine_kernel, "combine", [((TOK, D), BF), ((TOK, D), BF), ((TOK, 2), F32)],
        (back, hot_mine, hot_theirs, slots.T, combine, cotangent), 6 * TOK * SENT * D, 4 * MIB, 32)
    home, mixed, input_grad, combine_grad = lax.optimization_barrier((home, mixed, input_grad, combine_grad))
    rest = swap(lax.dynamic_index_in_dim(home, 1 - core, 1, keepdims=False), "c")
    grads = finish(at, half, across, home, rest)
    return mixed, input_grad, combine_grad, *grads


def solution(mesh):
    split = Mesh(mesh.devices.reshape(NZ, NXL, NY, NXH, NC), ALL)
    rows = P(ALL, None)
    owned = P(E, None, None)
    grads = P(E, None, ("xh", "c"))
    return jax.shard_map(
        per_device,
        mesh=split,
        in_specs=(rows, rows, rows, rows, P(), owned, owned, owned),
        out_specs=(rows, rows, rows, grads, grads, grads),
        check_vma=False,
    )
```

```python
import functools

import jax
import jax.numpy as jnp
from jax import lax
from jax.experimental import pallas as pl
from jax.experimental.pallas import tpu as pltpu
from jax.sharding import Mesh
from jax.sharding import PartitionSpec as P

D = 2048
H = 512
TOK = 128
EXPERTS = 64
CAP = 4
HOT_CAP = 12
SLOT = 2 * CAP
SENT = EXPERTS * SLOT
PAIR = 2 * HOT_CAP
SHARE = 128
WROWS = 3 * D
NZ, NXL, NY, NXH, NC = 8, 2, 4, 2, 2
ALL = ("z", "xl", "y", "xh", "c")
E = ("z", "xl", "y")
X = ("xl", "xh")
S = ("xl", "y")
PIECE = 32
BF = jnp.bfloat16
F32 = jnp.float32
MIB = 1024 * 1024


def contract(a, b, da, db):
    return lax.dot_general(a, b, (((da,), (db,)), ((), ())), preferred_element_type=F32)


def iota(shape, dim):
    return lax.broadcasted_iota(jnp.int32, shape, dim)


def cost(flops, nbytes):
    return pl.CostEstimate(flops=int(flops), bytes_accessed=int(nbytes), transcendentals=0)


def block_of(x):
    if x.ndim == 1:
        return pl.BlockSpec(memory_space=pltpu.SMEM)
    return pl.BlockSpec(x.shape, lambda i, n=x.ndim: (0,) * n)


def scalars(*values):
    return jnp.stack([jnp.asarray(v, jnp.int32) for v in values])


def call(kernel, name, out, args, flops=0, moved=2 * MIB, vmem=24, scratch=()):
    outs = tuple(jax.ShapeDtypeStruct(shape, dtype) for shape, dtype in out)
    return pl.pallas_call(
        kernel,
        grid=(1,),
        out_shape=outs,
        in_specs=[block_of(a) for a in args],
        out_specs=tuple(block_of(o) for o in outs),
        scratch_shapes=[pltpu.VMEM(shape, BF) for shape in scratch],
        compiler_params=pltpu.CompilerParams(vmem_limit_bytes=vmem * MIB),
        cost_estimate=cost(flops, moved),
        name=name,
    )(*args)


def onehot(mask):
    return mask.astype(F32).astype(BF)


def pack_kernel(at_ref, counts_ref, routes_ref, combine_ref, tokens_ref, cot_ref,
                send_ref, mine_ref, theirs_ref, slots_ref):
    core = at_ref[0]
    counts = counts_ref[...].astype(F32)
    ids = iota((1, EXPERTS), 1).astype(F32)
    low = jnp.float32(-3.0e38)

    def largest(values):
        top = jnp.max(values, axis=1, keepdims=True)
        return jnp.min(jnp.where(values == top, ids, float(EXPERTS)), axis=1, keepdims=True)

    hot0 = largest(counts)
    hot1 = largest(jnp.where(ids == hot0, low, counts))
    eid = iota((EXPERTS, TOK), 0)
    routes = [routes_ref[k:k + 1, :] for k in range(2)]
    weight = [combine_ref[k:k + 1, :] for k in range(2)]
    oh = [(eid == r).astype(F32) for r in routes]
    earlier = (iota((TOK, TOK), 0) < iota((TOK, TOK), 1)).astype(F32).astype(BF)
    cum = jnp.dot((oh[0] + oh[1]).astype(BF), earlier, preferred_element_type=F32)
    rank = [jnp.sum(cum * oh[0], axis=0, keepdims=True),
            jnp.sum((cum + oh[0]) * oh[1], axis=0, keepdims=True)]
    main, mine, theirs = [], [], []
    for k in range(2):
        rf = routes[k].astype(F32)
        lead = rf == hot0
        hot = lead | (rf == hot1)
        member = jnp.where(lead, 0, 1)
        r = rank[k].astype(jnp.int32)
        keep = r < jnp.where(hot, HOT_CAP, CAP)
        main.append(jnp.where(keep & jnp.logical_not(hot), routes[k] * SLOT + r, -1))
        mine.append(jnp.where(keep & hot & (member == core), r, -1))
        theirs.append(jnp.where(keep & hot & (member != core), r, -1))
        slots_ref[k:k + 1, :] = jnp.where(
            main[k] >= 0, main[k],
            jnp.where(mine[k] >= 0, SENT + mine[k], jnp.where(theirs[k] >= 0, SENT + PAIR + theirs[k], -1)))

    def rows(slot, shift, base, count):
        sid = iota((count, TOK), 0) + base
        at = [jnp.where(s >= 0, s + shift, -1) for s in slot]
        hit = [sid == s for s in slot]
        hit_c = [sid == a for a in at]
        pick = (hit[0] | hit[1]).astype(F32).astype(BF)
        pick_c = (hit_c[0] | hit_c[1]).astype(F32).astype(BF)
        w = jnp.sum(jnp.where(hit_c[0], weight[0], 0.0) + jnp.where(hit_c[1], weight[1], 0.0),
                    axis=1, keepdims=True)
        data = jnp.dot(pick, tokens_ref[...], preferred_element_type=F32)
        cot = jnp.dot(pick_c, cot_ref[...], preferred_element_type=F32)
        return (data + w * cot).astype(BF)

    mine_ref[...] = rows(mine, HOT_CAP, 0, PAIR)
    theirs_ref[...] = rows(theirs, HOT_CAP, 0, PAIR)
    step = 128

    def body(i, carry):
        base = pl.multiple_of(i * step, step)
        send_ref[pl.ds(base, step), :] = rows(main, CAP, base, step)
        return carry

    lax.fori_loop(0, SENT // step, body, 0)


def pack(at, counts, routes_t, combine_t, tokens, cotangent):
    out = [((SENT, D), BF), ((PAIR, D), BF), ((PAIR, D), BF), ((2, TOK), jnp.int32)]
    return call(pack_kernel, "pack", out, (at, counts, routes_t, combine_t, tokens, cotangent),
                4 * SENT * TOK * D, 4 * SENT * D, 32)


def backward_parts(gate, up, back):
    s = jax.nn.sigmoid(gate)
    act = (gate * s * up).astype(BF)
    gate_part = (back * up * s * (1.0 + gate * (1.0 - s))).astype(BF)
    up_part = (back * gate * s).astype(BF)
    return gate_part, up_part, act


def expert_kernel(got_ref, gate_ref, up_ref, down_ref, back_ref, data_ref, cot_ref, parts_ref):
    count = EXPERTS * CAP
    i, j = iota((count, SENT), 0), iota((count, SENT), 1)
    at = (i >> 2) * SLOT + (i & 3)
    data_ref[...] = jnp.dot((j == at).astype(F32).astype(BF), got_ref[...], preferred_element_type=F32).astype(BF)
    cot_ref[...] = jnp.dot((j == at + CAP).astype(F32).astype(BF), got_ref[...], preferred_element_type=F32).astype(BF)
    data, cot = data_ref[...], cot_ref[...]
    gate = jnp.dot(data, gate_ref[0], preferred_element_type=F32)
    up = jnp.dot(data, up_ref[0], preferred_element_type=F32)
    back = jnp.dot(cot, down_ref[0], preferred_element_type=F32)
    gate_part, up_part, act = backward_parts(gate, up, back)
    for m, part in enumerate((gate_part, up_part, act)):
        for q in range(H // SHARE):
            parts_ref[m, q] = part[:, q * SHARE:(q + 1) * SHARE]
    out = contract(act, down_ref[0], 1, 1).astype(BF)
    inp = (contract(gate_part, gate_ref[0], 1, 1) + contract(up_part, up_ref[0], 1, 1)).astype(BF)
    i, j = iota((SENT, count), 1), iota((SENT, count), 0)
    at = (i >> 2) * SLOT + (i & 3)
    back_ref[...] = (jnp.dot((j == at).astype(F32).astype(BF), out, preferred_element_type=F32)
                     + jnp.dot((j == at + CAP).astype(F32).astype(BF), inp, preferred_element_type=F32)).astype(BF)


def run_expert(got, weights):
    count = EXPERTS * CAP
    out = [((SENT, D), BF), ((count, D), BF), ((count, D), BF), ((3, H // SHARE, count, SHARE), BF)]
    return call(expert_kernel, "expert", out, (got,) + weights,
                12 * count * D * H + 8 * SENT * count * D, 12 * MIB, 56)


def grads_kernel(core_ref, data_ref, cot_ref, parts_ref, keep_ref, send_ref):
    core = core_ref[0]
    order = (core, 2 + core, 1 - core, 3 - core)
    pick = [[parts_ref[m, q] for q in order] for m in range(3)]
    first = contract(data_ref[...], jnp.concatenate(pick[0] + pick[1], axis=1), 0, 0)
    second = contract(cot_ref[...], jnp.concatenate(pick[2], axis=1), 0, 0)
    for m in range(3):
        for n in range(4):
            at = ((m * 4 + n) if m < 2 else n) * SHARE
            value = (first if m < 2 else second)[:, at:at + SHARE]
            if n < 2:
                keep_ref[n, m] = value
            else:
                send_ref[n - 2, m] = value.astype(BF)


def main_grads(core, data, cot, parts):
    count = EXPERTS * CAP
    block = 512
    return pl.pallas_call(
        grads_kernel,
        grid=(D // block,),
        out_shape=(jax.ShapeDtypeStruct((2, 3, D, SHARE), F32), jax.ShapeDtypeStruct((2, 3, D, SHARE), BF)),
        in_specs=[pl.BlockSpec(memory_space=pltpu.SMEM),
                  pl.BlockSpec((count, block), lambda i: (0, i)),
                  pl.BlockSpec((count, block), lambda i: (0, i)),
                  pl.BlockSpec((3, H // SHARE, count, SHARE), lambda i: (0, 0, 0, 0))],
        out_specs=(pl.BlockSpec((2, 3, block, SHARE), lambda i: (0, 0, i, 0)),
                   pl.BlockSpec((2, 3, block, SHARE), lambda i: (0, 0, i, 0))),
        compiler_params=pltpu.CompilerParams(vmem_limit_bytes=40 * MIB),
        cost_estimate=cost(6 * count * D * H, 12 * MIB),
        name="main_grads",
    )(core, data, cot, parts)


def cut_kernel(at_ref, gate_ref, up_ref, down_ref, *refs):
    out_refs, turned_ref = refs[:8], refs[8]
    xl, y = at_ref[2], at_ref[3]
    for m, ref in enumerate((gate_ref, up_ref, down_ref)):
        turned_ref[m] = ref[0].T
    for k, out_ref in enumerate(out_refs):
        start = ((xl + k // NY) & 1) * SHARE + ((y + k % NY) & 3) * PIECE
        rows = pl.ds(pl.multiple_of(start, PIECE), PIECE)
        for z in range(NZ):
            for m in range(3):
                out_ref[z, m] = turned_ref[m, rows, z * SHARE:(z + 1) * SHARE]


def cut_weights(at, weights):
    block = (NZ, 3, PIECE, SHARE)
    return pl.pallas_call(
        cut_kernel,
        out_shape=(jax.ShapeDtypeStruct(block, BF),) * 8,
        grid_spec=pltpu.PrefetchScalarGridSpec(
            num_scalar_prefetch=1,
            grid=(1,),
            in_specs=[pl.BlockSpec((1, D // 2, 2 * SHARE), lambda i, s: (0, s[0], s[1]))] * 3,
            out_specs=(pl.BlockSpec(block, lambda i, s: (0, 0, 0, 0)),) * 8,
            scratch_shapes=[pltpu.VMEM((3, 2 * SHARE, D // 2), BF)]),
        compiler_params=pltpu.CompilerParams(vmem_limit_bytes=24 * MIB),
        cost_estimate=cost(0, 5 * MIB),
        name="cut_weights",
    )(at, *weights)


def pick_plane_kernel(at_ref, *refs):
    ins, outs = refs[:8], refs[8:]
    z = at_ref[2]
    for m in range(2):
        for k in range(8):
            @pl.when(at_ref[m] == k)
            def _():
                for d in range(NZ):
                    outs[d][m] = ins[k][(z + d) & 7]


def pick_depth_kernel(at_ref, *refs):
    ins, (own_ref, other_ref) = refs[:8], refs[8:]
    core = at_ref[2]
    for d in range(NZ):
        @pl.when(at_ref[0] == d)
        def _():
            own_ref[...] = ins[d][core]

        @pl.when(at_ref[1] == d)
        def _():
            other_ref[...] = ins[d][1 - core]


def hot_kernel(at_ref, r0, r1, r2, r3, w0, w1, w2, w3, w4, w5, w6, w7, o0, o1, o2, o3, *refs):
    grad_refs, (weights_ref, data_ref, cot_ref, grads_ref) = refs[:8], refs[8:]
    z = at_ref[0]
    for d, ref in enumerate((w0, w1, w2, w3, w4, w5, w6, w7)):
        for half in range(2):
            cols = pl.ds(pl.multiple_of(half * (D // 2) + ((z - d) & 7) * SHARE, SHARE), SHARE)
            for m in range(3):
                weights_ref[m * PIECE:(m + 1) * PIECE, cols] = ref[half, m]
    total = 8 * PAIR
    count = total // 2

    def place(i):
        group = jnp.floor((i.astype(F32) + 0.5) * (1.0 / HOT_CAP)).astype(jnp.int32)
        return group * HOT_CAP + i

    i, j = iota((count, total), 0), iota((count, total), 1)
    at = place(i)
    pick, pick_c = onehot(j == at), onehot(j == at + HOT_CAP)
    for n, ref in enumerate((r0, r1, r2, r3)):
        rows = slice(n * count, (n + 1) * count)
        data_ref[rows, :] = jnp.dot(pick, ref[...], preferred_element_type=F32).astype(BF)
        cot_ref[rows, :] = jnp.dot(pick_c, ref[...], preferred_element_type=F32).astype(BF)
    data, cot = data_ref[...], cot_ref[...]
    both_w, down_w = weights_ref[0:2 * PIECE, :], weights_ref[2 * PIECE:3 * PIECE, :]
    gate = contract(data, weights_ref[0:PIECE, :], 1, 1)
    up = contract(data, weights_ref[PIECE:2 * PIECE, :], 1, 1)
    back = contract(cot, down_w, 1, 1)
    gate_part, up_part, act = backward_parts(gate, up, back)
    both = jnp.concatenate([gate_part, up_part], axis=1)
    out = jnp.dot(act, down_w, preferred_element_type=F32).astype(BF)
    inp = jnp.dot(both, both_w, preferred_element_type=F32).astype(BF)
    grads_ref[0:2 * PIECE, :] = contract(both, data, 0, 0).astype(BF)
    grads_ref[2 * PIECE:3 * PIECE, :] = contract(act, cot, 0, 0).astype(BF)
    width = D // NZ
    for d, ref in enumerate(grad_refs):
        cols = pl.ds(pl.multiple_of(((z + d) & 7) * width, width), width)
        for m in range(3):
            ref[m] = grads_ref[m * PIECE:(m + 1) * PIECE, cols]
    i, j = iota((total, count), 1), iota((total, count), 0)
    at = place(i)
    pick, pick_c = onehot(j == at), onehot(j == at + HOT_CAP)
    for n, ref in enumerate((o0, o1, o2, o3)):
        rows = slice(n * count, (n + 1) * count)
        ref[...] = (jnp.dot(pick, out[rows, :], preferred_element_type=F32)
                    + jnp.dot(pick_c, inp[rows, :], preferred_element_type=F32)).astype(BF)


def run_hot(at, rows, weights):
    total = 8 * PAIR
    out = [((total, D), BF)] * 4 + [((3, PIECE, D // NZ), BF)] * 8
    return call(hot_kernel, "hot", out, (at, *rows, *weights), 72 * total * D * PIECE, 8 * MIB, 48,
                ((3 * PIECE, D), (2 * total, D), (2 * total, D), (3 * PIECE, D)))


def sum_plane_kernel(p0, p1, p2, p3, *out_refs):
    size = 2 * PAIR
    for n, out_ref in enumerate(out_refs):
        rows = slice(n * size, (n + 1) * size)
        out_ref[...] = ((p0[rows, :].astype(F32) + p1[rows, :].astype(F32))
                        + (p2[rows, :].astype(F32) + p3[rows, :].astype(F32))).astype(BF)


def sum_rows_kernel(p0, p1, p2, p3, out_ref):
    out_ref[...] = ((p0[...].astype(F32) + p1[...].astype(F32))
                    + (p2[...].astype(F32) + p3[...].astype(F32))).astype(BF)


def sum_z_kernel(at_ref, *refs):
    ins, (keep_ref, give_ref) = refs[:8], refs[8:]
    core = at_ref[0]
    for ref, half in ((keep_ref, core), (give_ref, 1 - core)):
        cols = pl.ds(pl.multiple_of(half * SHARE, SHARE), SHARE)
        total = ins[0][:, :, cols].astype(F32)
        for part in ins[1:]:
            total = total + part[:, :, cols].astype(F32)
        ref[...] = total.astype(BF)


def combine_kernel(back_ref, mine_ref, theirs_ref, slots_ref, combine_ref, cot_ref,
                   mixed_ref, input_ref, cgrad_ref):
    slot = [slots_ref[:, k:k + 1] for k in range(2)]

    def pick(base, count, shift):
        lane = iota((TOK, count), 1) + (base - shift)
        inside = iota((TOK, count), 1) >= shift
        return [jnp.where((lane == s) & (s >= base) & inside, 1.0, 0.0) for s in slot]

    tables = ((back_ref, 0, SENT, CAP), (mine_ref, SENT, PAIR, HOT_CAP), (theirs_ref, SENT + PAIR, PAIR, HOT_CAP))
    outs = []
    for k in range(2):
        total = None
        for ref, base, count, shift in tables:
            term = jnp.dot(pick(base, count, 0)[k].astype(BF), ref[...], preferred_element_type=F32)
            total = term if total is None else total + term
        outs.append(total)
    total = None
    for ref, base, count, shift in tables:
        both = pick(base, count, shift)
        term = jnp.dot((both[0] + both[1]).astype(BF), ref[...], preferred_element_type=F32)
        total = term if total is None else total + term
    input_ref[...] = total.astype(BF)
    mixed_ref[...] = (combine_ref[:, 0:1] * outs[0] + combine_ref[:, 1:2] * outs[1]).astype(BF)
    cot = cot_ref[...].astype(F32)
    for k in range(2):
        cgrad_ref[:, k:k + 1] = jnp.sum(outs[k] * cot, axis=1, keepdims=True)


def finish_kernel(at_ref, part_ref, other_ref, got_ref, recv_ref, *out_refs):
    core = at_ref[0]
    eye = onehot(iota((SHARE, SHARE), 0) == iota((SHARE, SHARE), 1))
    for half in range(2):
        rows = pl.ds(pl.multiple_of((core if half == 0 else 1 - core) * SHARE, SHARE), SHARE)
        for m in range(3):
            piece = jnp.concatenate(
                [got_ref[0, 0, y, m] if half == 0 else recv_ref[0, y, m] for y in range(NY)], axis=0)
            out_refs[m][0, rows, :] = (part_ref[0, m, rows, :] + other_ref[m, rows, :].astype(F32)
                                       + contract(eye, piece, 1, 1))


def finish(at, half, across, home, rest):
    block = 2 * SHARE
    return pl.pallas_call(
        finish_kernel,
        out_shape=(jax.ShapeDtypeStruct((1, D, SHARE), F32),) * 3,
        grid_spec=pltpu.PrefetchScalarGridSpec(
            num_scalar_prefetch=1,
            grid=(NZ,),
            in_specs=[pl.BlockSpec((1, 3, block, SHARE), lambda i, s: (s[1], 0, i, 0)),
                      pl.BlockSpec((3, block, SHARE), lambda i, s: (0, i, 0)),
                      pl.BlockSpec((1, 1, NY, 3, PIECE, SHARE), lambda i, s: (i, s[0], 0, 0, 0, 0)),
                      pl.BlockSpec((1, NY, 3, PIECE, SHARE), lambda i, s: (i, 0, 0, 0, 0))],
            out_specs=(pl.BlockSpec((1, block, SHARE), lambda i, s: (0, i, 0)),) * 3),
        compiler_params=pltpu.CompilerParams(vmem_limit_bytes=24 * MIB),
        cost_estimate=cost(0, 10 * MIB),
        name="finish",
    )(at, half, across, home, rest)


def exchange(x, axes):
    return lax.all_to_all(x, axes, split_axis=0, concat_axis=0, tiled=True)


def swap(x, axis):
    return lax.ppermute(x, axis, [(0, 1), (1, 0)])


def shift(x, axis, size, d):
    return lax.ppermute(x, axis, [(i, (i + d) % size) for i in range(size)])


def shift_plane(x, k):
    return lax.ppermute(x, S, [(a * NY + b, (a ^ (k // NY)) * NY + (b + k % NY) % NY)
                               for a in range(NXL) for b in range(NY)])


def flip_x(x, m):
    return lax.ppermute(x, X, [(i, i ^ m) for i in range(4)])


def per_device(tokens, cotangent, routes, combine, counts, gate_weight, up_weight, down_weight):
    z, xl, y, xh, core = (lax.axis_index(a) for a in ALL)
    at = scalars(core, xh, xl, y, z)
    weights = (gate_weight, up_weight, down_weight)
    ids = jnp.arange(EXPERTS, dtype=jnp.int32)
    root0 = jnp.argmax(counts).astype(jnp.int32)
    root1 = jnp.argmax(jnp.where(ids == root0, jnp.iinfo(jnp.int32).min, counts)).astype(jnp.int32)
    rz, rxl, ry = zip(*((r // (NXL * NY), (r // NY) % NXL, r % NY) for r in (root0, root1)))
    first = core == 0

    cut = cut_weights(at, weights)
    plane = [cut[0]] + [shift_plane(cut[k], k) for k in range(1, 8)]
    send, mine, theirs, slots = pack(at, counts.reshape(1, EXPERTS), routes.T, combine.T, tokens, cotangent)
    ring = jnp.concatenate([mine, swap(theirs, "c")], axis=0)
    ring = jnp.concatenate([ring] + [flip_x(ring, m) for m in range(1, 4)], axis=0)
    plane, ring = lax.optimization_barrier((plane, ring))
    from_plane = [(xl ^ rxl[m]) * NY + ((y - ry[m]) & 3) for m in range(2)]
    depth = call(pick_plane_kernel, "pick_plane", [((2, 3, PIECE, SHARE), BF)] * 8,
                 (scalars(from_plane[0], from_plane[1], z), *plane))
    depth = [depth[0]] + [shift(depth[d], "z", NZ, d) for d in range(1, NZ)]
    hot_rows = [ring] + [shift(ring, "y", NY, d) for d in range(1, NY)]
    far = [(z - rz[m]) & 7 for m in range(2)]
    own, other = call(pick_depth_kernel, "pick_depth", [((3, PIECE, SHARE), BF)] * 2,
                      (scalars(jnp.where(first, far[0], far[1]), jnp.where(first, far[1], far[0]), core), *depth))
    other = swap(other, "c")
    piece = jnp.where(first, jnp.stack([own, other]), jnp.stack([other, own]))
    pieces = [piece] + [shift(piece, "z", NZ, d) for d in range(1, NZ)]

    send, pieces, hot_rows = lax.optimization_barrier((send, pieces, hot_rows))
    got = exchange(send, E)
    made = run_hot(z.reshape(1), hot_rows, pieces)
    by_y = [made[0]] + [shift(made[d], "y", NY, NY - d) for d in range(1, NY)]
    by_z = [made[4]] + [shift(made[4 + d], "z", NZ, d) for d in range(1, NZ)]
    ret = call(sum_plane_kernel, "sum_plane", [((2 * PAIR, D), BF)] * 4, by_y)
    own, other = call(sum_z_kernel, "sum_z", [((3, PIECE, SHARE), BF)] * 2, (core.reshape(1), *by_z))
    other = swap(other, "c")
    dest = iota((EXPERTS, 1, 1, 1), 0)
    home = jnp.where(dest == jnp.where(first, root0, root1), own[None],
                     jnp.where(dest == jnp.where(first, root1, root0), other[None], jnp.zeros((), BF)))

    home, got, ret = lax.optimization_barrier((home, got, ret))
    home = exchange(home.reshape(-1, SHARE), E).reshape(NZ, NXL, NY, 3, PIECE, SHARE)
    back, data, cot, parts = run_expert(got, weights)
    ret = [ret[0]] + [flip_x(ret[m], m) for m in range(1, 4)]
    hot_back, = call(sum_rows_kernel, "sum_rows", [((2 * PAIR, D), BF)], ret)
    hot_mine = hot_back[:PAIR]
    hot_theirs = swap(hot_back[PAIR:], "c")
    back, home, hot_theirs = lax.optimization_barrier((back, home, hot_theirs))
    back = exchange(back, E)
    keep, give = main_grads(at, data, cot, parts)
    half = keep + swap(give, "c").astype(F32)
    across = swap(lax.dynamic_index_in_dim(half, 1 - xh, 0, keepdims=False).astype(BF), "xh")
    rest = swap(lax.dynamic_index_in_dim(home, 1 - core, 1, keepdims=False), "c")
    grads = finish(at, half, across, home, rest)
    back, grads = lax.optimization_barrier((back, grads))
    mixed, input_grad, combine_grad = call(
        combine_kernel, "combine", [((TOK, D), BF), ((TOK, D), BF), ((TOK, 2), F32)],
        (back, hot_mine, hot_theirs, slots.T, combine, cotangent), 6 * TOK * SENT * D, 4 * MIB, 32)
    return mixed, input_grad, combine_grad, *grads


def solution(mesh):
    split = Mesh(mesh.devices.reshape(NZ, NXL, NY, NXH, NC), ALL)
    rows = P(ALL, None)
    owned = P(E, None, None)
    grads = P(E, None, ("xh", "c"))
    return jax.shard_map(
        per_device,
        mesh=split,
        in_specs=(rows, rows, rows, rows, P(), owned, owned, owned),
        out_specs=(rows, rows, rows, grads, grads, grads),
        check_vma=False,
    )
```

```python
import functools

import jax
import jax.numpy as jnp
from jax import lax
from jax.experimental import pallas as pl
from jax.experimental.pallas import tpu as pltpu
from jax.sharding import Mesh
from jax.sharding import PartitionSpec as P

D = 2048
H = 512
TOK = 128
EXPERTS = 64
CAP = 4
HOT_CAP = 12
SLOT = 2 * CAP
SENT = EXPERTS * SLOT
PAIR = 2 * HOT_CAP
SHARE = 128
WROWS = 3 * D
NZ, NXL, NY, NXH, NC = 8, 2, 4, 2, 2
ALL = ("z", "xl", "y", "xh", "c")
E = ("z", "xl", "y")
X = ("xl", "xh")
S = ("xl", "y")
PIECE = 32
BF = jnp.bfloat16
F32 = jnp.float32
MIB = 1024 * 1024


def contract(a, b, da, db):
    return lax.dot_general(a, b, (((da,), (db,)), ((), ())), preferred_element_type=F32)


def iota(shape, dim):
    return lax.broadcasted_iota(jnp.int32, shape, dim)


def cost(flops, nbytes):
    return pl.CostEstimate(flops=int(flops), bytes_accessed=int(nbytes), transcendentals=0)


def block_of(x):
    if x.ndim == 1:
        return pl.BlockSpec(memory_space=pltpu.SMEM)
    return pl.BlockSpec(x.shape, lambda i, n=x.ndim: (0,) * n)


def scalars(*values):
    return jnp.stack([jnp.asarray(v, jnp.int32) for v in values])


def call(kernel, name, out, args, flops=0, moved=2 * MIB, vmem=24, scratch=()):
    outs = tuple(jax.ShapeDtypeStruct(shape, dtype) for shape, dtype in out)
    return pl.pallas_call(
        kernel,
        grid=(1,),
        out_shape=outs,
        in_specs=[block_of(a) for a in args],
        out_specs=tuple(block_of(o) for o in outs),
        scratch_shapes=[pltpu.VMEM(shape, BF) for shape in scratch],
        compiler_params=pltpu.CompilerParams(vmem_limit_bytes=vmem * MIB),
        cost_estimate=cost(flops, moved),
        name=name,
    )(*args)


def onehot(mask):
    return mask.astype(F32).astype(BF)


def pack_kernel(at_ref, counts_ref, routes_ref, combine_ref, tokens_ref, cot_ref,
                send_ref, mine_ref, theirs_ref, slots_ref):
    core = at_ref[0]
    counts = counts_ref[...].astype(F32)
    ids = iota((1, EXPERTS), 1).astype(F32)
    low = jnp.float32(-3.0e38)

    def largest(values):
        top = jnp.max(values, axis=1, keepdims=True)
        return jnp.min(jnp.where(values == top, ids, float(EXPERTS)), axis=1, keepdims=True)

    hot0 = largest(counts)
    hot1 = largest(jnp.where(ids == hot0, low, counts))
    eid = iota((EXPERTS, TOK), 0)
    routes = [routes_ref[k:k + 1, :] for k in range(2)]
    weight = [combine_ref[k:k + 1, :] for k in range(2)]
    oh = [(eid == r).astype(F32) for r in routes]
    earlier = (iota((TOK, TOK), 0) < iota((TOK, TOK), 1)).astype(F32).astype(BF)
    cum = jnp.dot((oh[0] + oh[1]).astype(BF), earlier, preferred_element_type=F32)
    rank = [jnp.sum(cum * oh[0], axis=0, keepdims=True),
            jnp.sum((cum + oh[0]) * oh[1], axis=0, keepdims=True)]
    main, mine, theirs = [], [], []
    for k in range(2):
        rf = routes[k].astype(F32)
        lead = rf == hot0
        hot = lead | (rf == hot1)
        member = jnp.where(lead, 0, 1)
        r = rank[k].astype(jnp.int32)
        keep = r < jnp.where(hot, HOT_CAP, CAP)
        main.append(jnp.where(keep & jnp.logical_not(hot), routes[k] * SLOT + r, -1))
        mine.append(jnp.where(keep & hot & (member == core), r, -1))
        theirs.append(jnp.where(keep & hot & (member != core), r, -1))
        slots_ref[k:k + 1, :] = jnp.where(
            main[k] >= 0, main[k],
            jnp.where(mine[k] >= 0, SENT + mine[k], jnp.where(theirs[k] >= 0, SENT + PAIR + theirs[k], -1)))

    def rows(slot, shift, base, count):
        sid = iota((count, TOK), 0) + base
        at = [jnp.where(s >= 0, s + shift, -1) for s in slot]
        hit = [sid == s for s in slot]
        hit_c = [sid == a for a in at]
        pick = (hit[0] | hit[1]).astype(F32).astype(BF)
        pick_c = (hit_c[0] | hit_c[1]).astype(F32).astype(BF)
        w = jnp.sum(jnp.where(hit_c[0], weight[0], 0.0) + jnp.where(hit_c[1], weight[1], 0.0),
                    axis=1, keepdims=True)
        data = jnp.dot(pick, tokens_ref[...], preferred_element_type=F32)
        cot = jnp.dot(pick_c, cot_ref[...], preferred_element_type=F32)
        return (data + w * cot).astype(BF)

    mine_ref[...] = rows(mine, HOT_CAP, 0, PAIR)
    theirs_ref[...] = rows(theirs, HOT_CAP, 0, PAIR)
    step = 128

    def body(i, carry):
        base = pl.multiple_of(i * step, step)
        send_ref[pl.ds(base, step), :] = rows(main, CAP, base, step)
        return carry

    lax.fori_loop(0, SENT // step, body, 0)


def pack(at, counts, routes_t, combine_t, tokens, cotangent):
    out = [((SENT, D), BF), ((PAIR, D), BF), ((PAIR, D), BF), ((2, TOK), jnp.int32)]
    return call(pack_kernel, "pack", out, (at, counts, routes_t, combine_t, tokens, cotangent),
                4 * SENT * TOK * D, 4 * SENT * D, 32)


def backward_parts(gate, up, back):
    s = jax.nn.sigmoid(gate)
    act = (gate * s * up).astype(BF)
    gate_part = (back * up * s * (1.0 + gate * (1.0 - s))).astype(BF)
    up_part = (back * gate * s).astype(BF)
    return gate_part, up_part, act


def expert_kernel(got_ref, gate_ref, up_ref, down_ref, back_ref, data_ref, cot_ref, parts_ref):
    count = EXPERTS * CAP
    i, j = iota((count, SENT), 0), iota((count, SENT), 1)
    at = (i >> 2) * SLOT + (i & 3)
    data_ref[...] = jnp.dot((j == at).astype(F32).astype(BF), got_ref[...], preferred_element_type=F32).astype(BF)
    cot_ref[...] = jnp.dot((j == at + CAP).astype(F32).astype(BF), got_ref[...], preferred_element_type=F32).astype(BF)
    data, cot = data_ref[...], cot_ref[...]
    gate = jnp.dot(data, gate_ref[0], preferred_element_type=F32)
    up = jnp.dot(data, up_ref[0], preferred_element_type=F32)
    back = jnp.dot(cot, down_ref[0], preferred_element_type=F32)
    gate_part, up_part, act = backward_parts(gate, up, back)
    for m, part in enumerate((gate_part, up_part, act)):
        for q in range(H // SHARE):
            parts_ref[m, q] = part[:, q * SHARE:(q + 1) * SHARE]
    out = contract(act, down_ref[0], 1, 1).astype(BF)
    inp = (contract(gate_part, gate_ref[0], 1, 1) + contract(up_part, up_ref[0], 1, 1)).astype(BF)
    i, j = iota((SENT, count), 1), iota((SENT, count), 0)
    at = (i >> 2) * SLOT + (i & 3)
    back_ref[...] = (jnp.dot((j == at).astype(F32).astype(BF), out, preferred_element_type=F32)
                     + jnp.dot((j == at + CAP).astype(F32).astype(BF), inp, preferred_element_type=F32)).astype(BF)


def run_expert(got, weights):
    count = EXPERTS * CAP
    out = [((SENT, D), BF), ((count, D), BF), ((count, D), BF), ((3, H // SHARE, count, SHARE), BF)]
    return call(expert_kernel, "expert", out, (got,) + weights,
                12 * count * D * H + 8 * SENT * count * D, 12 * MIB, 56)


def grads_kernel(core_ref, data_ref, cot_ref, parts_ref, keep_ref, send_ref):
    core = core_ref[0]
    order = (core, 2 + core, 1 - core, 3 - core)
    pick = [[parts_ref[m, q] for q in order] for m in range(3)]
    first = contract(data_ref[...], jnp.concatenate(pick[0] + pick[1], axis=1), 0, 0)
    second = contract(cot_ref[...], jnp.concatenate(pick[2], axis=1), 0, 0)
    for m in range(3):
        for n in range(4):
            at = ((m * 4 + n) if m < 2 else n) * SHARE
            value = (first if m < 2 else second)[:, at:at + SHARE]
            if n < 2:
                keep_ref[n, m] = value
            else:
                send_ref[n - 2, m] = value.astype(BF)


def main_grads(core, data, cot, parts):
    count = EXPERTS * CAP
    block = 512
    return pl.pallas_call(
        grads_kernel,
        grid=(D // block,),
        out_shape=(jax.ShapeDtypeStruct((2, 3, D, SHARE), F32), jax.ShapeDtypeStruct((2, 3, D, SHARE), BF)),
        in_specs=[pl.BlockSpec(memory_space=pltpu.SMEM),
                  pl.BlockSpec((count, block), lambda i: (0, i)),
                  pl.BlockSpec((count, block), lambda i: (0, i)),
                  pl.BlockSpec((3, H // SHARE, count, SHARE), lambda i: (0, 0, 0, 0))],
        out_specs=(pl.BlockSpec((2, 3, block, SHARE), lambda i: (0, 0, i, 0)),
                   pl.BlockSpec((2, 3, block, SHARE), lambda i: (0, 0, i, 0))),
        compiler_params=pltpu.CompilerParams(vmem_limit_bytes=40 * MIB),
        cost_estimate=cost(6 * count * D * H, 12 * MIB),
        name="main_grads",
    )(core, data, cot, parts)


def cut_kernel(at_ref, gate_ref, up_ref, down_ref, *refs):
    out_refs, turned_ref = refs[:8], refs[8]
    xl, y = at_ref[2], at_ref[3]
    for m, ref in enumerate((gate_ref, up_ref, down_ref)):
        turned_ref[m] = ref[0].T
    for k, out_ref in enumerate(out_refs):
        start = ((xl + k // NY) & 1) * SHARE + ((y + k % NY) & 3) * PIECE
        rows = pl.ds(pl.multiple_of(start, PIECE), PIECE)
        for z in range(NZ):
            for m in range(3):
                out_ref[z, m] = turned_ref[m, rows, z * SHARE:(z + 1) * SHARE]


def cut_weights(at, weights):
    block = (NZ, 3, PIECE, SHARE)
    return pl.pallas_call(
        cut_kernel,
        out_shape=(jax.ShapeDtypeStruct(block, BF),) * 8,
        grid_spec=pltpu.PrefetchScalarGridSpec(
            num_scalar_prefetch=1,
            grid=(1,),
            in_specs=[pl.BlockSpec((1, D // 2, 2 * SHARE), lambda i, s: (0, s[0], s[1]))] * 3,
            out_specs=(pl.BlockSpec(block, lambda i, s: (0, 0, 0, 0)),) * 8,
            scratch_shapes=[pltpu.VMEM((3, 2 * SHARE, D // 2), BF)]),
        compiler_params=pltpu.CompilerParams(vmem_limit_bytes=24 * MIB),
        cost_estimate=cost(0, 5 * MIB),
        name="cut_weights",
    )(at, *weights)


def pick_plane_kernel(at_ref, *refs):
    ins, outs = refs[:8], refs[8:]
    z = at_ref[2]
    for m in range(2):
        for k in range(8):
            @pl.when(at_ref[m] == k)
            def _():
                for d in range(NZ):
                    outs[d][m] = ins[k][(z + d) & 7]


def pick_depth_kernel(at_ref, *refs):
    ins, (own_ref, other_ref) = refs[:8], refs[8:]
    core = at_ref[2]
    for d in range(NZ):
        @pl.when(at_ref[0] == d)
        def _():
            own_ref[...] = ins[d][core]

        @pl.when(at_ref[1] == d)
        def _():
            other_ref[...] = ins[d][1 - core]


def hot_kernel(at_ref, r0, r1, r2, r3, w0, w1, w2, w3, w4, w5, w6, w7, o0, o1, o2, o3, *refs):
    grad_refs, (weights_ref, data_ref, cot_ref, grads_ref) = refs[:8], refs[8:]
    z = at_ref[0]
    for d, ref in enumerate((w0, w1, w2, w3, w4, w5, w6, w7)):
        for half in range(2):
            cols = pl.ds(pl.multiple_of(half * (D // 2) + ((z - d) & 7) * SHARE, SHARE), SHARE)
            for m in range(3):
                weights_ref[m * PIECE:(m + 1) * PIECE, cols] = ref[half, m]
    total = 8 * PAIR
    count = total // 2

    def place(i):
        group = jnp.floor((i.astype(F32) + 0.5) * (1.0 / HOT_CAP)).astype(jnp.int32)
        return group * HOT_CAP + i

    i, j = iota((count, total), 0), iota((count, total), 1)
    at = place(i)
    pick, pick_c = onehot(j == at), onehot(j == at + HOT_CAP)
    for n, ref in enumerate((r0, r1, r2, r3)):
        rows = slice(n * count, (n + 1) * count)
        data_ref[rows, :] = jnp.dot(pick, ref[...], preferred_element_type=F32).astype(BF)
        cot_ref[rows, :] = jnp.dot(pick_c, ref[...], preferred_element_type=F32).astype(BF)
    data, cot = data_ref[...], cot_ref[...]
    both_w, down_w = weights_ref[0:2 * PIECE, :], weights_ref[2 * PIECE:3 * PIECE, :]
    gate = contract(data, weights_ref[0:PIECE, :], 1, 1)
    up = contract(data, weights_ref[PIECE:2 * PIECE, :], 1, 1)
    back = contract(cot, down_w, 1, 1)
    gate_part, up_part, act = backward_parts(gate, up, back)
    both = jnp.concatenate([gate_part, up_part], axis=1)
    out = jnp.dot(act, down_w, preferred_element_type=F32).astype(BF)
    inp = jnp.dot(both, both_w, preferred_element_type=F32).astype(BF)
    grads_ref[0:2 * PIECE, :] = contract(both, data, 0, 0).astype(BF)
    grads_ref[2 * PIECE:3 * PIECE, :] = contract(act, cot, 0, 0).astype(BF)
    width = D // NZ
    for d, ref in enumerate(grad_refs):
        cols = pl.ds(pl.multiple_of(((z + d) & 7) * width, width), width)
        for m in range(3):
            ref[m] = grads_ref[m * PIECE:(m + 1) * PIECE, cols]
    i, j = iota((total, count), 1), iota((total, count), 0)
    at = place(i)
    pick, pick_c = onehot(j == at), onehot(j == at + HOT_CAP)
    for n, ref in enumerate((o0, o1, o2, o3)):
        rows = slice(n * count, (n + 1) * count)
        ref[...] = (jnp.dot(pick, out[rows, :], preferred_element_type=F32)
                    + jnp.dot(pick_c, inp[rows, :], preferred_element_type=F32)).astype(BF)


def run_hot(at, rows, weights):
    total = 8 * PAIR
    out = [((total, D), BF)] * 4 + [((3, PIECE, D // NZ), BF)] * 8
    return call(hot_kernel, "hot", out, (at, *rows, *weights), 72 * total * D * PIECE, 8 * MIB, 48,
                ((3 * PIECE, D), (2 * total, D), (2 * total, D), (3 * PIECE, D)))


def sum_plane_kernel(p0, p1, p2, p3, *out_refs):
    size = 2 * PAIR
    for n, out_ref in enumerate(out_refs):
        rows = slice(n * size, (n + 1) * size)
        out_ref[...] = ((p0[rows, :].astype(F32) + p1[rows, :].astype(F32))
                        + (p2[rows, :].astype(F32) + p3[rows, :].astype(F32))).astype(BF)


def sum_rows_kernel(p0, p1, p2, p3, out_ref):
    out_ref[...] = ((p0[...].astype(F32) + p1[...].astype(F32))
                    + (p2[...].astype(F32) + p3[...].astype(F32))).astype(BF)


def sum_z_kernel(at_ref, *refs):
    ins, (keep_ref, give_ref) = refs[:8], refs[8:]
    core = at_ref[0]
    for ref, half in ((keep_ref, core), (give_ref, 1 - core)):
        cols = pl.ds(pl.multiple_of(half * SHARE, SHARE), SHARE)
        total = ins[0][:, :, cols].astype(F32)
        for part in ins[1:]:
            total = total + part[:, :, cols].astype(F32)
        ref[...] = total.astype(BF)


def combine_kernel(back_ref, mine_ref, theirs_ref, slots_ref, combine_ref, cot_ref,
                   mixed_ref, input_ref, cgrad_ref):
    slot = [slots_ref[:, k:k + 1] for k in range(2)]

    def pick(base, count, shift):
        lane = iota((TOK, count), 1) + (base - shift)
        inside = iota((TOK, count), 1) >= shift
        return [jnp.where((lane == s) & (s >= base) & inside, 1.0, 0.0) for s in slot]

    tables = ((back_ref, 0, SENT, CAP), (mine_ref, SENT, PAIR, HOT_CAP), (theirs_ref, SENT + PAIR, PAIR, HOT_CAP))
    outs = []
    for k in range(2):
        total = None
        for ref, base, count, shift in tables:
            term = jnp.dot(pick(base, count, 0)[k].astype(BF), ref[...], preferred_element_type=F32)
            total = term if total is None else total + term
        outs.append(total)
    total = None
    for ref, base, count, shift in tables:
        both = pick(base, count, shift)
        term = jnp.dot((both[0] + both[1]).astype(BF), ref[...], preferred_element_type=F32)
        total = term if total is None else total + term
    input_ref[...] = total.astype(BF)
    mixed_ref[...] = (combine_ref[:, 0:1] * outs[0] + combine_ref[:, 1:2] * outs[1]).astype(BF)
    cot = cot_ref[...].astype(F32)
    for k in range(2):
        cgrad_ref[:, k:k + 1] = jnp.sum(outs[k] * cot, axis=1, keepdims=True)


def finish_kernel(at_ref, part_ref, other_ref, got_ref, recv_ref, *out_refs):
    core = at_ref[0]
    eye = onehot(iota((SHARE, SHARE), 0) == iota((SHARE, SHARE), 1))
    for half in range(2):
        rows = pl.ds(pl.multiple_of((core if half == 0 else 1 - core) * SHARE, SHARE), SHARE)
        for m in range(3):
            piece = jnp.concatenate(
                [got_ref[0, 0, y, m] if half == 0 else recv_ref[0, y, m] for y in range(NY)], axis=0)
            out_refs[m][0, rows, :] = (part_ref[0, m, rows, :] + other_ref[m, rows, :].astype(F32)
                                       + contract(eye, piece, 1, 1))


def finish(at, half, across, home, rest):
    block = 2 * SHARE
    return pl.pallas_call(
        finish_kernel,
        out_shape=(jax.ShapeDtypeStruct((1, D, SHARE), F32),) * 3,
        grid_spec=pltpu.PrefetchScalarGridSpec(
            num_scalar_prefetch=1,
            grid=(NZ,),
            in_specs=[pl.BlockSpec((1, 3, block, SHARE), lambda i, s: (s[1], 0, i, 0)),
                      pl.BlockSpec((3, block, SHARE), lambda i, s: (0, i, 0)),
                      pl.BlockSpec((1, 1, NY, 3, PIECE, SHARE), lambda i, s: (i, s[0], 0, 0, 0, 0)),
                      pl.BlockSpec((1, NY, 3, PIECE, SHARE), lambda i, s: (i, 0, 0, 0, 0))],
            out_specs=(pl.BlockSpec((1, block, SHARE), lambda i, s: (0, i, 0)),) * 3),
        compiler_params=pltpu.CompilerParams(vmem_limit_bytes=24 * MIB),
        cost_estimate=cost(0, 10 * MIB),
        name="finish",
    )(at, half, across, home, rest)


def exchange(x, axes):
    return lax.all_to_all(x, axes, split_axis=0, concat_axis=0, tiled=True)


def swap(x, axis):
    return lax.ppermute(x, axis, [(0, 1), (1, 0)])


def shift(x, axis, size, d):
    return lax.ppermute(x, axis, [(i, (i + d) % size) for i in range(size)])


def shift_plane(x, k):
    return lax.ppermute(x, S, [(a * NY + b, (a ^ (k // NY)) * NY + (b + k % NY) % NY)
                               for a in range(NXL) for b in range(NY)])


def flip_x(x, m):
    return lax.ppermute(x, X, [(i, i ^ m) for i in range(4)])


def per_device(tokens, cotangent, routes, combine, counts, gate_weight, up_weight, down_weight):
    z, xl, y, xh, core = (lax.axis_index(a) for a in ALL)
    at = scalars(core, xh, xl, y, z)
    weights = (gate_weight, up_weight, down_weight)
    ids = jnp.arange(EXPERTS, dtype=jnp.int32)
    root0 = jnp.argmax(counts).astype(jnp.int32)
    root1 = jnp.argmax(jnp.where(ids == root0, jnp.iinfo(jnp.int32).min, counts)).astype(jnp.int32)
    rz, rxl, ry = zip(*((r // (NXL * NY), (r // NY) % NXL, r % NY) for r in (root0, root1)))
    first = core == 0

    send, mine, theirs, slots = pack(at, counts.reshape(1, EXPERTS), routes.T, combine.T, tokens, cotangent)
    got = exchange(send, E)

    cut = cut_weights(at, weights)
    plane = [cut[0]] + [shift_plane(cut[k], k) for k in range(1, 8)]
    from_plane = [(xl ^ rxl[m]) * NY + ((y - ry[m]) & 3) for m in range(2)]
    ring = jnp.concatenate([mine, swap(theirs, "c")], axis=0)
    ring = jnp.concatenate([ring] + [flip_x(ring, m) for m in range(1, 4)], axis=0)
    plane, ring = lax.optimization_barrier((plane, ring))
    depth = call(pick_plane_kernel, "pick_plane", [((2, 3, PIECE, SHARE), BF)] * 8,
                 (scalars(from_plane[0], from_plane[1], z), *plane))
    depth = [depth[0]] + [shift(depth[d], "z", NZ, d) for d in range(1, NZ)]

    hot_rows = [ring] + [shift(ring, "y", NY, d) for d in range(1, NY)]

    far = [(z - rz[m]) & 7 for m in range(2)]
    own, other = call(pick_depth_kernel, "pick_depth", [((3, PIECE, SHARE), BF)] * 2,
                      (scalars(jnp.where(first, far[0], far[1]), jnp.where(first, far[1], far[0]), core), *depth))
    other = swap(other, "c")
    piece = jnp.where(first, jnp.stack([own, other]), jnp.stack([other, own]))
    piece, hot_rows, got = lax.optimization_barrier((piece, hot_rows, got))
    pieces = [piece] + [shift(piece, "z", NZ, d) for d in range(1, NZ)]

    back, data, cot, parts = run_expert(got, weights)
    back, pieces = lax.optimization_barrier((back, pieces))
    back = exchange(back, E)

    made = run_hot(z.reshape(1), hot_rows, pieces)
    (data, cot, parts), made = lax.optimization_barrier(((data, cot, parts), made))
    by_z = [made[4]] + [shift(made[4 + d], "z", NZ, d) for d in range(1, NZ)]
    by_y = [made[0]] + [shift(made[d], "y", NY, NY - d) for d in range(1, NY)]
    ret = call(sum_plane_kernel, "sum_plane", [((2 * PAIR, D), BF)] * 4, by_y)
    by_z, ret = lax.optimization_barrier((by_z, ret))
    ret = [ret[0]] + [flip_x(ret[m], m) for m in range(1, 4)]
    hot_back, = call(sum_rows_kernel, "sum_rows", [((2 * PAIR, D), BF)], ret)
    hot_mine = hot_back[:PAIR]
    hot_theirs = swap(hot_back[PAIR:], "c")

    keep, give = main_grads(at, data, cot, parts)
    half = keep + swap(give, "c").astype(F32)
    across = swap(lax.dynamic_index_in_dim(half, 1 - xh, 0, keepdims=False).astype(BF), "xh")

    own, other = call(sum_z_kernel, "sum_z", [((3, PIECE, SHARE), BF)] * 2, (core.reshape(1), *by_z))
    other = swap(other, "c")
    dest = iota((EXPERTS, 1, 1, 1), 0)
    home = jnp.where(dest == jnp.where(first, root0, root1), own[None],
                     jnp.where(dest == jnp.where(first, root1, root0), other[None], jnp.zeros((), BF)))
    home, back = lax.optimization_barrier((home, back))
    home, _ = lax.optimization_barrier((home, across))
    home = exchange(home.reshape(-1, SHARE), E).reshape(NZ, NXL, NY, 3, PIECE, SHARE)

    mixed, input_grad, combine_grad = call(
        combine_kernel, "combine", [((TOK, D), BF), ((TOK, D), BF), ((TOK, 2), F32)],
        (back, hot_mine, hot_theirs, slots.T, combine, cotangent), 6 * TOK * SENT * D, 4 * MIB, 32)
    home, mixed, input_grad, combine_grad = lax.optimization_barrier((home, mixed, input_grad, combine_grad))
    rest = swap(lax.dynamic_index_in_dim(home, 1 - core, 1, keepdims=False), "c")
    grads = finish(at, half, across, home, rest)
    return mixed, input_grad, combine_grad, *grads


def solution(mesh):
    split = Mesh(mesh.devices.reshape(NZ, NXL, NY, NXH, NC), ALL)
    rows = P(ALL, None)
    owned = P(E, None, None)
    grads = P(E, None, ("xh", "c"))
    return jax.shard_map(
        per_device,
        mesh=split,
        in_specs=(rows, rows, rows, rows, P(), owned, owned, owned),
        out_specs=(rows, rows, rows, grads, grads, grads),
        check_vma=False,
    )
```
